128 devices in a mesh: gx: 16 (over y, x), gy: 4 (over z), gz: 2 (over core).
Axes of the slice: x: 4, y: 4, z: 4, core: 2. Of those that a mesh axis runs over, the one named last changes fastest.
Arguments:
- velocity: float32 [3, 32, 256, 8192], P(None, 'gz', 'gx', 'gy'), may hold values from -6 to 6
- blade_pos: float32 [256, 3, 128], P(('gx', 'gy', 'gz')), as said below
- block_turbine: int32 [256], P(('gx', 'gy', 'gz')), may hold values from 0 to 3, as said below
- blade_vel: float32 [256, 3, 128], P(('gx', 'gy', 'gz')), may hold values from -6 to 6
- lift_coeff: float32 [256, 128], P(('gx', 'gy', 'gz')), may hold values from 0.2 to 2
Outputs:
- new_velocity: float32 [3, 32, 256, 8192], P(None, 'gz', 'gx', 'gy')
- point_force: float32 [256, 3, 128], P(('gx', 'gy', 'gz'))
The draws below stay inside these ranges and needn't reach their ends.
Inputs may be any that keep to these rules, and one draw needn't show every extreme that they name: `block_turbine`: in each turbine row (blocks r * 4 * 2 * 2 onward, one row for each index of gx) every turbine number is named by exactly 4 blocks. `blade_pos`: the points of a block lie in its column: streamwise within its row's cells, spanwise within its turbine's cells, vertically between level 0 and the top level.
All inputs are finite; a program needn't handle non-finite values.
Results may differ from the reference program's by a relative error of at most 0.0003.
Values sent between devices are 32-bit elements; how exact they have to be, the bound alone decides.
A program may use at most 192 MiB of HBM per device.

```python
import math
import jax
import jax.numpy as jnp
from jax import lax

CX = 16
CY = 2048
PTS = 128
BLK_OWN = 2
NX = 256
NY = 8192
NZ = 32
BLOCKS = 256
N_GX = 16
N_GY = 4
N_GZ = 2


def turbine_ids(key):
    row_blocks = N_GY * N_GZ * BLK_OWN
    row_keys = jax.random.split(jax.random.fold_in(key, 21), N_GX)
    shuffled = jax.vmap(lambda one_key: jax.random.permutation(one_key, row_blocks))(row_keys)
    return (shuffled // (N_GZ * BLK_OWN)).astype(jnp.int32).reshape(N_GX * row_blocks)


def draw_block_turbine(key, part):
    return turbine_ids(key)


def draw_blade_pos(key, part):
    turbine = turbine_ids(key).astype(jnp.float32)
    row = (jnp.arange(BLOCKS, dtype=jnp.int32) // (N_GY * N_GZ * BLK_OWN)).astype(jnp.float32)
    unit_x = jax.random.uniform(jax.random.fold_in(key, 22), (BLOCKS, PTS), jnp.float32)
    unit_y = jax.random.uniform(jax.random.fold_in(key, 23), (BLOCKS, PTS), jnp.float32)
    unit_z = jax.random.uniform(jax.random.fold_in(key, 24), (BLOCKS, PTS), jnp.float32)
    coord_x = row[:, None] * CX + unit_x * (CX - 1)
    coord_y = turbine[:, None] * CY + unit_y * (CY - 1)
    coord_z = unit_z * (NZ - 1)
    return jnp.stack([coord_x, coord_y, coord_z], axis=1).astype(jnp.float32)


def smooth_mean(key, strength):
    level = jnp.arange(NZ, dtype=jnp.int32).astype(jnp.float32) / max(NZ - 1, 1)
    stream = jnp.arange(NX, dtype=jnp.int32).astype(jnp.float32) / NX
    phase = jax.random.uniform(jax.random.fold_in(key, 2), (3,), jnp.float32, 0.0, 2.0 * math.pi)
    height = 0.85 + 0.3 * level
    wave = 1.0 + 0.1 * jnp.sin(2.0 * math.pi * stream[None, :] + phase[:, None])
    return strength[:, None, None, None] * height[None, :, None, None] * wave[:, None, :, None]


def draw_velocity(key, part):
    key = jax.random.fold_in(key, 31)
    shape = (3, NZ, NX, NY)
    strength = jnp.array([3.0, 2.5, -2.0], jnp.float32)
    noise = jax.random.normal(jax.random.fold_in(key, 1), shape, jnp.float32)
    field = smooth_mean(key, strength) + noise
    return jnp.clip(field, -6.0, 6.0).astype(jnp.float32)


def block_levels(own_key, shape, cuts, least, largest):
    gain, own = 1.0, jax.random.fold_in(own_key, 6)
    for axis_at, blocks in cuts:
        heights = jnp.exp(jax.random.uniform(jax.random.fold_in(own, axis_at), (blocks,), jnp.float32, least / len(cuts), largest / len(cuts)))
        gain = gain * jnp.repeat(heights, shape[axis_at] // blocks).reshape([-1 if axis == axis_at else 1 for axis in range(len(shape))])
    return gain


def normal_values(key, dims, scale, limit, pieces=(), held_as=jnp.bfloat16):
    drawn = scale * jax.random.normal(key, dims, jnp.float32)
    if pieces:
        drawn = drawn * block_levels(key, dims, pieces, -0.22, 0.18)
    return jnp.clip(drawn, -limit, limit).astype(held_as)


def setup_inputs(seed: int = 0) -> dict:
    arg_keys = jax.random.split(jax.random.key(seed), 6)
    return {
        "velocity": draw_velocity(jax.random.fold_in(arg_keys[5], 71), 0),
        "blade_pos": draw_blade_pos(jax.random.fold_in(arg_keys[5], 71), 0),
        "block_turbine": draw_block_turbine(jax.random.fold_in(arg_keys[5], 71), 0),
        "blade_vel": normal_values(arg_keys[3], (BLOCKS, 3, PTS), 1.0, 6.0, ((0, 128),), jnp.float32),
        "lift_coeff": jnp.clip(jnp.exp(math.log(2.0) - 2.3025851 * jax.random.uniform(arg_keys[4], (BLOCKS, PTS), jnp.float32) ** block_levels(arg_keys[4], (BLOCKS, PTS), ((0, 128),), -0.2, 0.2)), 0.2, 2.0),
    }


mean_wind = 1.0
viscosity = 0.2
smag_coeff = 0.17
time_step = 0.2
smear = 2.0
smear_norm = 1.0 / (smear ** 3 * math.pi ** 1.5)

def shifted(padded, axis_dim, offset):
    slicer = [slice(None), slice(2, -2), slice(2, -2), slice(2, -2)]
    extent = padded.shape[axis_dim] - 4
    slicer[axis_dim] = slice(2 + offset, 2 + offset + extent)
    return padded[tuple(slicer)]

def derivative(padded, axis_dim):
    near = shifted(padded, axis_dim, 1) - shifted(padded, axis_dim, -1)
    far = shifted(padded, axis_dim, 2) - shifted(padded, axis_dim, -2)
    return (8.0 * near - far) / 12.0

def second(padded, axis_dim):
    return (-shifted(padded, axis_dim, 2) + 16.0 * shifted(padded, axis_dim, 1) - 30.0 * shifted(padded, axis_dim, 0) + 16.0 * shifted(padded, axis_dim, -1) - shifted(padded, axis_dim, -2)) / 12.0

def tendency(padded, body_force):
    along_x = derivative(padded, 2)
    along_y = derivative(padded, 3)
    along_z = derivative(padded, 1)
    gradients = (along_x, along_y, along_z)
    strain_sq = jnp.zeros(along_x.shape[1:], jnp.float32)
    for row_comp in range(3):
        for col_comp in range(3):
            strain = 0.5 * (gradients[col_comp][row_comp] + gradients[row_comp][col_comp])
            strain_sq = strain_sq + strain * strain
    eddy_visc = smag_coeff * smag_coeff * jnp.sqrt(2.0 * strain_sq)
    laplacian = second(padded, 1) + second(padded, 2) + second(padded, 3)
    return -mean_wind * along_x + (viscosity + eddy_visc[None]) * laplacian + body_force

def blade_force(sampled, blade_vel, lift_coeff):
    relative = sampled - blade_vel
    rel_speed = jnp.sqrt(lax.optimization_barrier(jnp.sum(relative * relative, axis=1, keepdims=True)))
    return -lift_coeff[:, None, :] * rel_speed * relative

def profile(anchor, count, centers):
    cells = (anchor + jnp.arange(count, dtype=jnp.int32)).astype(jnp.float32)
    gap = cells[:, None] - centers[None, :]
    return jnp.exp(-gap * gap / (smear * smear))

def column_weights(centers, row, turbine):
    wx = profile(row * CX, CX, centers[0])
    wy = profile(turbine * CY, CY, centers[1])
    wz = profile(0, NZ, centers[2])
    zx = (wz[:, None, :] * wx[None, :, :]).reshape(NZ * CX, centers.shape[1])
    return (zx, wy)

def reference(velocity, blade_pos, block_turbine, blade_vel, lift_coeff):
    high = lax.Precision.HIGHEST
    row_blocks = N_GY * N_GZ * BLK_OWN
    per_turbine = N_GZ * BLK_OWN
    count = per_turbine * PTS
    turbines = block_turbine.reshape(N_GX, row_blocks).astype(jnp.int32)
    order = jnp.argsort(turbines, axis=1, stable=True).astype(jnp.int32).reshape(N_GX, N_GY, per_turbine)
    positions = blade_pos.reshape(N_GX, row_blocks, 3, PTS)
    row_vel = velocity.reshape(3, NZ, N_GX, CX, NY).transpose(2, 0, 1, 3, 4)
    rows = jnp.arange(N_GX, dtype=jnp.int32)

    def sample_row(items):
        row, vel_row, order_row, pos_row = items
        result = jnp.zeros((row_blocks, 3, PTS), jnp.float32)
        for turbine in range(N_GY):
            picked = order_row[turbine]
            centers = pos_row[picked].transpose(1, 0, 2).reshape(3, count)
            zx, wy = column_weights(centers, row, turbine)
            column = vel_row[:, :, :, turbine * CY:(turbine + 1) * CY].reshape(3 * NZ * CX, CY)
            along = jnp.dot(column, wy, precision=high, preferred_element_type=jnp.float32).reshape(3, NZ * CX, count)
            partial_value = smear_norm * lax.optimization_barrier(jnp.sum(along * zx[None], axis=1))
            partial_value = partial_value.reshape(3, per_turbine, PTS).transpose(1, 0, 2)
            result = result.at[picked].set(partial_value)
        return result
    sampled = lax.map(sample_row, (rows, row_vel, order, positions)).reshape(BLOCKS, 3, PTS)
    point_force = blade_force(sampled, blade_vel, lift_coeff)
    row_force = point_force.reshape(N_GX, row_blocks, 3, PTS)

    def spread_row(items):
        row, order_row, pos_row, force_row = items
        columns = []
        for turbine in range(N_GY):
            picked = order_row[turbine]
            centers = pos_row[picked].transpose(1, 0, 2).reshape(3, count)
            zx, wy = column_weights(centers, row, turbine)
            flat = force_row[picked].transpose(1, 0, 2).reshape(3, count)
            weighted = (smear_norm * flat[:, None, :] * zx[None]).reshape(3 * NZ * CX, count)
            spread = lax.dot_general(weighted, wy, (((1,), (1,)), ((), ())), precision=high, preferred_element_type=jnp.float32)
            columns.append(spread.reshape(3, NZ, CX, CY))
        return jnp.concatenate(columns, axis=3)
    body_rows = lax.map(spread_row, (rows, order, positions, row_force))
    body_force = body_rows.transpose(1, 2, 0, 3, 4).reshape(3, NZ, NX, NY)
    padded = jnp.pad(velocity, ((0, 0), (2, 2), (2, 2), (2, 2)))
    new_velocity = velocity + time_step * tendency(padded, body_force)
    return (new_velocity, point_force)
```

```python
import functools
import math

import jax
import jax.numpy as jnp
from jax import lax
from jax.experimental import pallas as pl
from jax.experimental.pallas import tpu as pltpu
from jax.sharding import PartitionSpec as P

mean_wind = 1.0
viscosity = 0.2
smag_coeff = 0.17
time_step = 0.2
smear = 2.0
smear_norm = 1.0 / (smear**3 * math.pi**1.5)

F32, BF16 = jnp.float32, jnp.bfloat16
MESH = pl.DeviceIdType.MESH
LANES = 128
TOP = 8


def split(value):
    high = value.astype(BF16)
    return high, (value - high.astype(F32)).astype(BF16)


def gaussian(start, count, centers):
    cells = (lax.broadcasted_iota(jnp.int32, (count, 1), 0) + start).astype(F32)
    gap = cells - centers
    return jnp.exp(gap * gap * (-1.0 / (smear * smear)))


def stencil(win, tile, z, body):
    lane = lax.broadcasted_iota(jnp.int32, (16, LANES), 1)
    grads, laps, own = [], [], []
    for c in range(3):
        def rows(offset, level=0, side=0, c=c):
            return win[tile + side, c, z + level, TOP + offset : TOP + offset + 16, :]

        u = rows(0)
        left, right = rows(0, side=-1), rows(0, side=1)
        y_p1 = pltpu.roll(jnp.where(lane < 1, right, u), LANES - 1, 1)
        y_p2 = pltpu.roll(jnp.where(lane < 2, right, u), LANES - 2, 1)
        y_m1 = pltpu.roll(jnp.where(lane >= LANES - 1, left, u), 1, 1)
        y_m2 = pltpu.roll(jnp.where(lane >= LANES - 2, left, u), 2, 1)
        pairs = (
            (rows(1), rows(-1), rows(2), rows(-2)),
            (y_p1, y_m1, y_p2, y_m2),
            (rows(0, 1), rows(0, -1), rows(0, 2), rows(0, -2)),
        )
        grads.append([8.0 * (p1 - m1) - (p2 - m2) for p1, m1, p2, m2 in pairs])
        near = sum(p1 + m1 for p1, m1, _, _ in pairs[1:]) + (pairs[0][0] + pairs[0][1])
        far = sum(p2 + m2 for _, _, p2, m2 in pairs[1:]) + (pairs[0][2] + pairs[0][3])
        laps.append(16.0 * near - far - 90.0 * u)
        own.append(u)
    diag = sum(grads[i][i] * grads[i][i] for i in range(3))
    cross = jnp.zeros((16, LANES), F32)
    for i, j in ((0, 1), (0, 2), (1, 2)):
        both = grads[i][j] + grads[j][i]
        cross = cross + both * both
    strain = diag + diag + cross
    nu = viscosity * time_step / 12.0 + (smag_coeff * smag_coeff * time_step / 144.0) * jnp.sqrt(strain)
    outs = []
    for c in range(3):
        outs.append(own[c] + (-mean_wind * time_step / 12.0) * grads[c][0] + nu * laps[c] + time_step * body[c])
    return outs


def kernel(
    sizes, v, pos, turb, bvel, lift, out, pf,
    win, table, whi, wlo, along, plane, ghi, glo, part, other, back, owned,
    load_sem, tab_send, tab_recv, z_send, z_recv, x_send, x_recv, y_send, y_recv,
    part_sem, back_send, back_recv,
):
    n_gx, n_gy, n_gz = sizes
    gx, gy, gz = lax.axis_index("gx"), lax.axis_index("gy"), lax.axis_index("gz")
    mine = gy * n_gz + gz
    group = n_gy * n_gz
    _, depth, nrow, ncol = v.shape
    tiles = ncol // LANES
    own_blocks = pos.shape[0]
    blocks = group * own_blocks
    per_turbine = blocks // n_gy
    pts = pos.shape[2]
    count = per_turbine * pts
    rows = 3 * depth * nrow

    barrier = pltpu.get_barrier_semaphore()
    for step in range(1, group):
        peer = lax.rem(mine + step, group)
        pl.semaphore_signal(
            barrier, 1, device_id={"gy": peer // n_gz, "gz": lax.rem(peer, n_gz)}, device_id_type=MESH
        )

    @pl.when(gx > 0)
    def _():
        pl.semaphore_signal(barrier, 1, device_id={"gx": gx - 1}, device_id_type=MESH)

    @pl.when(gx < n_gx - 1)
    def _():
        pl.semaphore_signal(barrier, 1, device_id={"gx": gx + 1}, device_id_type=MESH)

    def lanes(t):
        return pl.ds(pl.multiple_of(t * LANES, LANES), LANES)

    def load(t):
        return pltpu.make_async_copy(
            v.at[:, :, :, lanes(t)], win.at[t + 1, :, pl.ds(2, depth), pl.ds(TOP, nrow), :], load_sem.at[t]
        )

    @pl.loop(0, tiles)
    def _(t):
        load(t).start()

    for b in range(own_blocks):
        at = mine * own_blocks + b
        table[at, 0:3, :] = pos[b]
        table[at, 3:6, :] = bvel[b]
        table[at, 6:7, :] = lift[b : b + 1, :]
        table[at, 7:8, :] = jnp.full((1, pts), turb[b].astype(F32))

    z_gap = jnp.where(gz == 0, 0, depth + 2)

    @pl.loop(0, tiles)
    def _(t):
        for c in range(3):
            for k in range(2):
                win[t + 1, c, z_gap + k, TOP : TOP + nrow, :] = jnp.zeros((nrow, LANES), F32)

    @pl.when(gx == 0)
    def _():
        @pl.loop(0, tiles)
        def _(t):
            win[t + 1, :, 2 : 2 + depth, TOP - 2 : TOP, :] = jnp.zeros((3, depth, 2, LANES), F32)

    @pl.when(gx == n_gx - 1)
    def _():
        @pl.loop(0, tiles)
        def _(t):
            win[t + 1, :, 2 : 2 + depth, TOP + nrow : TOP + nrow + 2, :] = jnp.zeros((3, depth, 2, LANES), F32)

    @pl.when(gy == 0)
    def _():
        win[0, :, 2 : 2 + depth, TOP : TOP + nrow, :] = jnp.zeros((3, depth, nrow, LANES), F32)

    @pl.when(gy == n_gy - 1)
    def _():
        win[tiles + 1, :, 2 : 2 + depth, TOP : TOP + nrow, :] = jnp.zeros((3, depth, nrow, LANES), F32)

    pl.semaphore_wait(barrier, group - 1 + (gx > 0).astype(jnp.int32) + (gx < n_gx - 1).astype(jnp.int32))

    def remote(src, dst, send, recv, device):
        return pltpu.make_async_remote_copy(
            src_ref=src, dst_ref=dst, send_sem=send, recv_sem=recv, device_id=device, device_id_type=MESH
        )

    own_slots = pl.ds(mine * own_blocks, own_blocks)

    def tab(step):
        peer = lax.rem(mine + step, group)
        return remote(
            table.at[own_slots], table.at[own_slots], tab_send.at[step], tab_recv.at[step],
            {"gy": peer // n_gz, "gz": lax.rem(peer, n_gz)},
        )

    z_from = jnp.where(gz == 0, depth - 2, 0)
    z_to = jnp.where(gz == 0, 0, depth + 2)

    def z_copy(t):
        return remote(
            v.at[:, pl.ds(z_from, 2), :, lanes(t)],
            win.at[t + 1, :, pl.ds(z_to, 2), pl.ds(TOP, nrow), :],
            z_send.at[t], z_recv.at[t], {"gz": 1 - gz},
        )

    def x_up(t):
        return remote(
            v.at[:, :, pl.ds(nrow - 2, 2), lanes(t)],
            win.at[t + 1, :, pl.ds(2, depth), pl.ds(TOP - 2, 2), :],
            x_send.at[0, t], x_recv.at[0, t], {"gx": gx + 1},
        )

    def x_down(t):
        return remote(
            v.at[:, :, pl.ds(0, 2), lanes(t)],
            win.at[t + 1, :, pl.ds(2, depth), pl.ds(TOP + nrow, 2), :],
            x_send.at[1, t], x_recv.at[1, t], {"gx": gx - 1},
        )

    def y_copy(side):
        first = 0 if side else ncol - LANES
        return remote(
            v.at[:, :, :, pl.ds(first, LANES)],
            win.at[tiles + 1 if side else 0, :, pl.ds(2, depth), pl.ds(TOP, nrow), :],
            y_send.at[side], y_recv.at[side], {"gy": gy - 1 if side else gy + 1},
        )

    for step in range(1, group):
        tab(step).start()

    @pl.when(gy > 0)
    def _():
        y_copy(1).start()

    @pl.when(gy < n_gy - 1)
    def _():
        y_copy(0).start()

    @pl.loop(0, tiles)
    def _(t):
        @pl.when(gx < n_gx - 1)
        def _():
            x_up(t).start()

        @pl.when(gx > 0)
        def _():
            x_down(t).start()

        z_copy(t).start()

    for step in range(1, group):
        tab(step).wait_recv()
    turbine = gy.astype(F32)

    def matches():
        rank = jnp.zeros((8, pts), F32)
        for s in range(blocks):
            entry = table[s]
            match = jnp.broadcast_to(entry[7:8, :], (8, pts)) == turbine
            yield s, entry, [match & (rank == float(k)) for k in range(per_turbine)]
            rank = rank + jnp.where(match, 1.0, 0.0)

    slots = [jnp.zeros((8, pts), F32) for _ in range(per_turbine)]
    for _, entry, chosen in matches():
        slots = [jnp.where(one, entry, held) for one, held in zip(chosen, slots)]

    def flat(row):
        return jnp.concatenate([slot[row : row + 1, :] for slot in slots], axis=1)

    weight_x = gaussian(gx * nrow, nrow, flat(0))
    weight_z = gaussian(gz * depth, depth, flat(2))
    for z in range(depth):
        plane[z * nrow : (z + 1) * nrow, :] = weight_z[z : z + 1, :] * weight_x
    center_y = flat(1)

    step_cols = 2 * LANES
    steps = ncol // step_cols

    @pl.loop(0, steps)
    def _(j):
        at = pl.multiple_of(j * step_cols, step_cols)
        high, low = split(gaussian(gy * ncol + at, step_cols, center_y))
        whi[pl.ds(at, step_cols), :] = high
        wlo[pl.ds(at, step_cols), :] = low
        load(2 * j).wait()
        load(2 * j + 1).wait()
        cells = jnp.concatenate(
            [
                win[2 * j + 1 + k, :, 2 : 2 + depth, TOP : TOP + nrow, :].reshape(rows, LANES)
                for k in range(2)
            ],
            axis=1,
        )
        vhi, vlo = split(cells)
        dot = functools.partial(jnp.dot, preferred_element_type=F32)
        now = dot(vhi, high) + (dot(vhi, low) + dot(vlo, high))

        @pl.when(j == 0)
        def _():
            along[...] = now

        @pl.when(j > 0)
        def _():
            along[...] += now

    per_comp = depth * nrow
    part[3:8, :] = jnp.zeros((5, count), F32)
    for c in range(3):
        part[c : c + 1, :] = jnp.sum(
            along[c * per_comp : (c + 1) * per_comp, :] * plane[...], axis=0, keepdims=True
        )
    swap = remote(part, other, part_sem.at[0], part_sem.at[1], {"gz": 1 - gz})
    swap.start()
    swap.wait_recv()
    relative = [
        smear_norm * (part[c : c + 1, :] + other[c : c + 1, :]) - flat(3 + c) for c in range(3)
    ]
    speed = jnp.sqrt(relative[0] * relative[0] + relative[1] * relative[1] + relative[2] * relative[2])
    force = [-flat(6) * speed * relative[c] for c in range(3)]

    stacked = [
        jnp.concatenate(
            [force[c][:, k * pts : (k + 1) * pts] for c in range(3)] + [jnp.zeros((5, pts), F32)], axis=0
        )
        for k in range(per_turbine)
    ]
    for s, _, chosen in matches():
        back[s] = sum(jnp.where(one, held, 0.0) for one, held in zip(chosen, stacked))

    def give(step):
        peer = lax.rem(gy + step, n_gy)
        return remote(
            back.at[pl.ds((peer * n_gz + gz) * own_blocks, own_blocks)], owned.at[step],
            back_send.at[step], back_recv.at[step], {"gy": peer},
        )

    for step in range(1, n_gy):
        give(step).start()

    for c in range(3):
        high, low = split((smear_norm * force[c]) * plane[...])
        ghi[c * per_comp : (c + 1) * per_comp, :] = high
        glo[c * per_comp : (c + 1) * per_comp, :] = low

    @pl.when(gy > 0)
    def _():
        y_copy(0).wait_recv()

    @pl.when(gy < n_gy - 1)
    def _():
        y_copy(1).wait_recv()

    @pl.loop(0, steps)
    def _(j):
        at = pl.multiple_of(j * step_cols, step_cols)
        high, low = whi[pl.ds(at, step_cols), :], wlo[pl.ds(at, step_cols), :]

        def dot(a, b):
            return lax.dot_general(a, b, (((1,), (1,)), ((), ())), preferred_element_type=F32)

        along[:, 0:step_cols] = dot(ghi[...], high) + (dot(ghi[...], low) + dot(glo[...], high))
        for k in range(2):
            t = 2 * j + k

            @pl.when(gx > 0)
            def _():
                x_up(t).wait_recv()

            @pl.when(gx < n_gx - 1)
            def _():
                x_down(t).wait_recv()

            z_copy(t).wait_recv()

            @pl.loop(0, depth // 4)
            def _(zb):
                for dz in range(4):
                    z = zb * 4 + dz
                    body = [
                        along[
                            pl.ds(pl.multiple_of(c * per_comp + z * nrow, nrow), nrow),
                            k * LANES : (k + 1) * LANES,
                        ]
                        for c in range(3)
                    ]
                    new = stencil(win, t + 1, z + 2, body)
                    for c in range(3):
                        out[c, z, :, lanes(t)] = new[c]

    for step in range(1, n_gy):
        give(step).wait()
    total = back[own_slots] + sum(owned[step] for step in range(1, n_gy))
    pf[...] = total[:, 0:3, :]
    for step in range(1, group):
        tab(step).wait_send()
    swap.wait_send()

    @pl.when(gy > 0)
    def _():
        y_copy(1).wait_send()

    @pl.when(gy < n_gy - 1)
    def _():
        y_copy(0).wait_send()

    @pl.loop(0, tiles)
    def _(t):
        @pl.when(gx < n_gx - 1)
        def _():
            x_up(t).wait_send()

        @pl.when(gx > 0)
        def _():
            x_down(t).wait_send()

        z_copy(t).wait_send()


def local(sizes, velocity, blade_pos, block_turbine, blade_vel, lift_coeff):
    n_gx, n_gy, n_gz = sizes
    comps, depth, nrow, ncol = velocity.shape
    own_blocks, _, pts = blade_pos.shape
    tiles = ncol // LANES
    group = n_gy * n_gz
    blocks = group * own_blocks
    count = blocks // n_gy * pts
    rows = comps * depth * nrow
    dma = pltpu.SemaphoreType.DMA
    vmem = pl.BlockSpec(memory_space=pltpu.VMEM)
    return pl.pallas_call(
        functools.partial(kernel, sizes),
        out_shape=(
            jax.ShapeDtypeStruct(velocity.shape, F32),
            jax.ShapeDtypeStruct(blade_pos.shape, F32),
        ),
        in_specs=[
            pl.BlockSpec(memory_space=pl.ANY), vmem, pl.BlockSpec(memory_space=pltpu.SMEM), vmem, vmem,
        ],
        out_specs=(vmem, vmem),
        scratch_shapes=[
            pltpu.VMEM((tiles + 2, comps, depth + 4, nrow + 16, LANES), F32),
            pltpu.VMEM((blocks, 8, pts), F32),
            pltpu.VMEM((ncol, count), BF16),
            pltpu.VMEM((ncol, count), BF16),
            pltpu.VMEM((rows, count), F32),
            pltpu.VMEM((depth * nrow, count), F32),
            pltpu.VMEM((rows, count), BF16),
            pltpu.VMEM((rows, count), BF16),
            pltpu.VMEM((8, count), F32),
            pltpu.VMEM((8, count), F32),
            pltpu.VMEM((blocks, 8, pts), F32),
            pltpu.VMEM((n_gy, own_blocks, 8, pts), F32),
            dma((tiles,)),
            dma((group,)), dma((group,)),
            dma((tiles,)), dma((tiles,)),
            dma((2, tiles)), dma((2, tiles)),
            dma((2,)), dma((2,)),
            dma((2,)),
            dma((n_gy,)), dma((n_gy,)),
        ],
        compiler_params=pltpu.CompilerParams(
            collective_id=0, has_side_effects=True, vmem_limit_bytes=60 * 2**20
        ),
        name="evolve",
    )(velocity, blade_pos, block_turbine, blade_vel, lift_coeff)


def solution(mesh):
    sizes = tuple(mesh.shape[axis] for axis in ("gx", "gy", "gz"))
    in_specs = (
        P(None, "gz", "gx", "gy"),
        P(("gx", "gy", "gz"), None, None),
        P(("gx", "gy", "gz")),
        P(("gx", "gy", "gz"), None, None),
        P(("gx", "gy", "gz"), None),
    )
    out_specs = (P(None, "gz", "gx", "gy"), P(("gx", "gy", "gz"), None, None))
    return jax.shard_map(
        functools.partial(local, sizes), mesh=mesh, in_specs=in_specs, out_specs=out_specs, check_vma=False
    )
```

```python
import functools
import math

import jax
import jax.numpy as jnp
from jax import lax
from jax.experimental import pallas as pl
from jax.experimental.pallas import tpu as pltpu
from jax.sharding import PartitionSpec as P

mean_wind = 1.0
viscosity = 0.2
smag_coeff = 0.17
time_step = 0.2
smear = 2.0
smear_norm = 1.0 / (smear**3 * math.pi**1.5)

F32, BF16 = jnp.float32, jnp.bfloat16
MESH = pl.DeviceIdType.MESH
LANES = 128
TOP = 8


def split(value):
    high = value.astype(BF16)
    return high, (value - high.astype(F32)).astype(BF16)


def gaussian(start, count, centers):
    cells = (lax.broadcasted_iota(jnp.int32, (count, 1), 0) + start).astype(F32)
    gap = cells - centers
    return jnp.exp(gap * gap * (-1.0 / (smear * smear)))


def stencil(win, tile, z, body):
    lane = lax.broadcasted_iota(jnp.int32, (16, LANES), 1)
    grads, laps, own = [], [], []
    for c in range(3):
        def rows(offset, level=0, side=0, c=c):
            return win[tile + side, c, z + level, TOP + offset : TOP + offset + 16, :]

        u = rows(0)
        left, right = rows(0, side=-1), rows(0, side=1)
        y_p1 = pltpu.roll(jnp.where(lane < 1, right, u), LANES - 1, 1)
        y_p2 = pltpu.roll(jnp.where(lane < 2, right, u), LANES - 2, 1)
        y_m1 = pltpu.roll(jnp.where(lane >= LANES - 1, left, u), 1, 1)
        y_m2 = pltpu.roll(jnp.where(lane >= LANES - 2, left, u), 2, 1)
        pairs = (
            (rows(1), rows(-1), rows(2), rows(-2)),
            (y_p1, y_m1, y_p2, y_m2),
            (rows(0, 1), rows(0, -1), rows(0, 2), rows(0, -2)),
        )
        grads.append([8.0 * (p1 - m1) - (p2 - m2) for p1, m1, p2, m2 in pairs])
        near = sum(p1 + m1 for p1, m1, _, _ in pairs[1:]) + (pairs[0][0] + pairs[0][1])
        far = sum(p2 + m2 for _, _, p2, m2 in pairs[1:]) + (pairs[0][2] + pairs[0][3])
        laps.append(16.0 * near - far - 90.0 * u)
        own.append(u)
    diag = sum(grads[i][i] * grads[i][i] for i in range(3))
    cross = jnp.zeros((16, LANES), F32)
    for i, j in ((0, 1), (0, 2), (1, 2)):
        both = grads[i][j] + grads[j][i]
        cross = cross + both * both
    strain = diag + diag + cross
    nu = viscosity * time_step / 12.0 + (smag_coeff * smag_coeff * time_step / 144.0) * jnp.sqrt(strain)
    outs = []
    for c in range(3):
        outs.append(own[c] + (-mean_wind * time_step / 12.0) * grads[c][0] + nu * laps[c] + time_step * body[c])
    return outs


def kernel(
    sizes, v, pos_in, turb_in, bvel_in, lift_in, out, pf,
    pos, turb, bvel, lift,
    win, table, whi, wlo, along, plane, ghi, glo, part, other, back, owned,
    small_sem, load_sem, tab_send, tab_recv, z_send, z_recv, x_send, x_recv, y_send, y_recv,
    part_sem, back_send, back_recv,
):
    n_gx, n_gy, n_gz = sizes
    gx, gy, gz = lax.axis_index("gx"), lax.axis_index("gy"), lax.axis_index("gz")
    mine = gy * n_gz + gz
    group = n_gy * n_gz
    _, depth, nrow, ncol = v.shape
    tiles = ncol // LANES
    own_blocks = pos.shape[1]
    blocks = group * own_blocks
    per_turbine = blocks // n_gy
    pts = pos.shape[2]
    count = per_turbine * pts
    rows = 3 * depth * nrow

    small = [
        pltpu.make_async_copy(src, dst, small_sem.at[i])
        for i, (src, dst) in enumerate(((turb_in, turb), (pos_in, pos), (bvel_in, bvel), (lift_in, lift)))
    ]
    for copy in small:
        copy.start()

    barrier = pltpu.get_barrier_semaphore()
    for step in range(1, group):
        peer = lax.rem(mine + step, group)
        pl.semaphore_signal(
            barrier, 1, device_id={"gy": peer // n_gz, "gz": lax.rem(peer, n_gz)}, device_id_type=MESH
        )

    @pl.when(gx > 0)
    def _():
        pl.semaphore_signal(barrier, 1, device_id={"gx": gx - 1}, device_id_type=MESH)

    @pl.when(gx < n_gx - 1)
    def _():
        pl.semaphore_signal(barrier, 1, device_id={"gx": gx + 1}, device_id_type=MESH)

    def lanes(t):
        return pl.ds(pl.multiple_of(t * LANES, LANES), LANES)

    def load(t):
        return pltpu.make_async_copy(
            v.at[:, :, :, lanes(t)], win.at[t + 1, :, pl.ds(2, depth), pl.ds(TOP, nrow), :], load_sem.at[t]
        )

    @pl.loop(0, tiles)
    def _(t):
        load(t).start()

    for copy in small:
        copy.wait()
    for b in range(own_blocks):
        at = mine * own_blocks + b
        for c in range(3):
            table[at, c : c + 1, :] = pos[c, b : b + 1, :]
            table[at, 3 + c : 4 + c, :] = bvel[c, b : b + 1, :]
        table[at, 6:7, :] = lift[b : b + 1, :]
        table[at, 7:8, :] = jnp.full((1, pts), turb[b].astype(F32))

    z_gap = jnp.where(gz == 0, 0, depth + 2)

    @pl.loop(0, tiles)
    def _(t):
        for c in range(3):
            for k in range(2):
                win[t + 1, c, z_gap + k, TOP : TOP + nrow, :] = jnp.zeros((nrow, LANES), F32)

    @pl.when(gx == 0)
    def _():
        @pl.loop(0, tiles)
        def _(t):
            win[t + 1, :, 2 : 2 + depth, TOP - 2 : TOP, :] = jnp.zeros((3, depth, 2, LANES), F32)

    @pl.when(gx == n_gx - 1)
    def _():
        @pl.loop(0, tiles)
        def _(t):
            win[t + 1, :, 2 : 2 + depth, TOP + nrow : TOP + nrow + 2, :] = jnp.zeros((3, depth, 2, LANES), F32)

    @pl.when(gy == 0)
    def _():
        win[0, :, 2 : 2 + depth, TOP : TOP + nrow, :] = jnp.zeros((3, depth, nrow, LANES), F32)

    @pl.when(gy == n_gy - 1)
    def _():
        win[tiles + 1, :, 2 : 2 + depth, TOP : TOP + nrow, :] = jnp.zeros((3, depth, nrow, LANES), F32)

    pl.semaphore_wait(barrier, group - 1 + (gx > 0).astype(jnp.int32) + (gx < n_gx - 1).astype(jnp.int32))

    def remote(src, dst, send, recv, device):
        return pltpu.make_async_remote_copy(
            src_ref=src, dst_ref=dst, send_sem=send, recv_sem=recv, device_id=device, device_id_type=MESH
        )

    own_slots = pl.ds(mine * own_blocks, own_blocks)

    def tab(step):
        peer = lax.rem(mine + step, group)
        return remote(
            table.at[own_slots], table.at[own_slots], tab_send.at[step], tab_recv.at[step],
            {"gy": peer // n_gz, "gz": lax.rem(peer, n_gz)},
        )

    z_from = jnp.where(gz == 0, depth - 2, 0)
    z_to = jnp.where(gz == 0, 0, depth + 2)

    def z_copy(t):
        return remote(
            v.at[:, pl.ds(z_from, 2), :, lanes(t)],
            win.at[t + 1, :, pl.ds(z_to, 2), pl.ds(TOP, nrow), :],
            z_send.at[t], z_recv.at[t], {"gz": 1 - gz},
        )

    def x_up(t):
        return remote(
            v.at[:, :, pl.ds(nrow - 2, 2), lanes(t)],
            win.at[t + 1, :, pl.ds(2, depth), pl.ds(TOP - 2, 2), :],
            x_send.at[0, t], x_recv.at[0, t], {"gx": gx + 1},
        )

    def x_down(t):
        return remote(
            v.at[:, :, pl.ds(0, 2), lanes(t)],
            win.at[t + 1, :, pl.ds(2, depth), pl.ds(TOP + nrow, 2), :],
            x_send.at[1, t], x_recv.at[1, t], {"gx": gx - 1},
        )

    def y_copy(side):
        first = 0 if side else ncol - LANES
        return remote(
            v.at[:, :, :, pl.ds(first, LANES)],
            win.at[tiles + 1 if side else 0, :, pl.ds(2, depth), pl.ds(TOP, nrow), :],
            y_send.at[side], y_recv.at[side], {"gy": gy - 1 if side else gy + 1},
        )

    for step in range(1, group):
        tab(step).start()

    @pl.when(gy > 0)
    def _():
        y_copy(1).start()

    @pl.when(gy < n_gy - 1)
    def _():
        y_copy(0).start()

    @pl.loop(0, tiles)
    def _(t):
        @pl.when(gx < n_gx - 1)
        def _():
            x_up(t).start()

        @pl.when(gx > 0)
        def _():
            x_down(t).start()

        z_copy(t).start()

    for step in range(1, group):
        tab(step).wait_recv()
    turbine = gy.astype(F32)

    def matches():
        rank = jnp.zeros((8, pts), F32)
        for s in range(blocks):
            entry = table[s]
            match = jnp.broadcast_to(entry[7:8, :], (8, pts)) == turbine
            yield s, entry, [match & (rank == float(k)) for k in range(per_turbine)]
            rank = rank + jnp.where(match, 1.0, 0.0)

    slots = [jnp.zeros((8, pts), F32) for _ in range(per_turbine)]
    for _, entry, chosen in matches():
        slots = [jnp.where(one, entry, held) for one, held in zip(chosen, slots)]

    def flat(row):
        return jnp.concatenate([slot[row : row + 1, :] for slot in slots], axis=1)

    weight_x = gaussian(gx * nrow, nrow, flat(0))
    weight_z = gaussian(gz * depth, depth, flat(2))
    for z in range(depth):
        plane[z * nrow : (z + 1) * nrow, :] = weight_z[z : z + 1, :] * weight_x
    center_y = flat(1)

    step_cols = 2 * LANES
    steps = ncol // step_cols

    @pl.loop(0, steps)
    def _(j):
        at = pl.multiple_of(j * step_cols, step_cols)
        high, low = split(gaussian(gy * ncol + at, step_cols, center_y))
        whi[pl.ds(at, step_cols), :] = high
        wlo[pl.ds(at, step_cols), :] = low
        load(2 * j).wait()
        load(2 * j + 1).wait()
        cells = jnp.concatenate(
            [
                win[2 * j + 1 + k, :, 2 : 2 + depth, TOP : TOP + nrow, :].reshape(rows, LANES)
                for k in range(2)
            ],
            axis=1,
        )
        vhi, vlo = split(cells)
        dot = functools.partial(jnp.dot, preferred_element_type=F32)
        now = dot(vhi, high) + (dot(vhi, low) + dot(vlo, high))

        @pl.when(j == 0)
        def _():
            along[...] = now

        @pl.when(j > 0)
        def _():
            along[...] += now

    per_comp = depth * nrow
    part[3:8, :] = jnp.zeros((5, count), F32)
    for c in range(3):
        part[c : c + 1, :] = jnp.sum(
            along[c * per_comp : (c + 1) * per_comp, :] * plane[...], axis=0, keepdims=True
        )
    swap = remote(part, other, part_sem.at[0], part_sem.at[1], {"gz": 1 - gz})
    swap.start()
    swap.wait_recv()
    relative = [
        smear_norm * (part[c : c + 1, :] + other[c : c + 1, :]) - flat(3 + c) for c in range(3)
    ]
    speed = jnp.sqrt(relative[0] * relative[0] + relative[1] * relative[1] + relative[2] * relative[2])
    force = [-flat(6) * speed * relative[c] for c in range(3)]

    stacked = [
        jnp.concatenate(
            [force[c][:, k * pts : (k + 1) * pts] for c in range(3)] + [jnp.zeros((5, pts), F32)], axis=0
        )
        for k in range(per_turbine)
    ]
    for s, _, chosen in matches():
        back[s] = sum(jnp.where(one, held, 0.0) for one, held in zip(chosen, stacked))

    def give(step):
        peer = lax.rem(gy + step, n_gy)
        return remote(
            back.at[pl.ds((peer * n_gz + gz) * own_blocks, own_blocks)], owned.at[step],
            back_send.at[step], back_recv.at[step], {"gy": peer},
        )

    for step in range(1, n_gy):
        give(step).start()

    for c in range(3):
        high, low = split((smear_norm * force[c]) * plane[...])
        ghi[c * per_comp : (c + 1) * per_comp, :] = high
        glo[c * per_comp : (c + 1) * per_comp, :] = low

    @pl.when(gy > 0)
    def _():
        y_copy(0).wait_recv()

    @pl.when(gy < n_gy - 1)
    def _():
        y_copy(1).wait_recv()

    @pl.loop(0, steps)
    def _(j):
        at = pl.multiple_of(j * step_cols, step_cols)
        high, low = whi[pl.ds(at, step_cols), :], wlo[pl.ds(at, step_cols), :]

        def dot(a, b):
            return lax.dot_general(a, b, (((1,), (1,)), ((), ())), preferred_element_type=F32)

        along[:, 0:step_cols] = dot(ghi[...], high) + (dot(ghi[...], low) + dot(glo[...], high))
        for k in range(2):
            t = 2 * j + k

            @pl.when(gx > 0)
            def _():
                x_up(t).wait_recv()

            @pl.when(gx < n_gx - 1)
            def _():
                x_down(t).wait_recv()

            z_copy(t).wait_recv()

            @pl.loop(0, depth // 4)
            def _(zb):
                for dz in range(4):
                    z = zb * 4 + dz
                    body = [
                        along[
                            pl.ds(pl.multiple_of(c * per_comp + z * nrow, nrow), nrow),
                            k * LANES : (k + 1) * LANES,
                        ]
                        for c in range(3)
                    ]
                    new = stencil(win, t + 1, z + 2, body)
                    for c in range(3):
                        out[c, z, :, lanes(t)] = new[c]

    for step in range(1, n_gy):
        give(step).wait()
    total = back[own_slots] + sum(owned[step] for step in range(1, n_gy))
    for c in range(3):
        for b in range(own_blocks):
            pf[c, b : b + 1, :] = total[b, c : c + 1, :]
    for step in range(1, group):
        tab(step).wait_send()
    swap.wait_send()

    @pl.when(gy > 0)
    def _():
        y_copy(1).wait_send()

    @pl.when(gy < n_gy - 1)
    def _():
        y_copy(0).wait_send()

    @pl.loop(0, tiles)
    def _(t):
        @pl.when(gx < n_gx - 1)
        def _():
            x_up(t).wait_send()

        @pl.when(gx > 0)
        def _():
            x_down(t).wait_send()

        z_copy(t).wait_send()


def write_out(new, forces, new_out, forces_out, sem):
    copies = [pltpu.make_async_copy(forces, forces_out, sem.at[0])]
    for c in range(new.shape[0]):
        copies.append(pltpu.make_async_copy(new.at[c], new_out.at[c], sem.at[c + 1]))
    for copy in copies:
        copy.start()
    for copy in copies:
        copy.wait()


def local(sizes, velocity, blade_pos, block_turbine, blade_vel, lift_coeff):
    n_gx, n_gy, n_gz = sizes
    comps, depth, nrow, ncol = velocity.shape
    own_blocks, _, pts = blade_pos.shape
    tiles = ncol // LANES
    group = n_gy * n_gz
    blocks = group * own_blocks
    count = blocks // n_gy * pts
    rows = comps * depth * nrow
    dma = pltpu.SemaphoreType.DMA
    vmem = pl.BlockSpec(memory_space=pltpu.VMEM)
    by_comp = (blade_pos.shape[1], own_blocks, pts)
    made = pl.pallas_call(
        functools.partial(kernel, sizes),
        out_shape=(pltpu.VMEM(velocity.shape, F32), pltpu.VMEM(by_comp, F32)),
        in_specs=[pl.BlockSpec(memory_space=pl.ANY)] * 5,
        out_specs=(vmem, vmem),
        scratch_shapes=[
            pltpu.VMEM(by_comp, F32),
            pltpu.SMEM((own_blocks,), jnp.int32),
            pltpu.VMEM(by_comp, F32),
            pltpu.VMEM((own_blocks, pts), F32),
            pltpu.VMEM((tiles + 2, comps, depth + 4, nrow + 16, LANES), F32),
            pltpu.VMEM((blocks, 8, pts), F32),
            pltpu.VMEM((ncol, count), BF16),
            pltpu.VMEM((ncol, count), BF16),
            pltpu.VMEM((rows, count), F32),
            pltpu.VMEM((depth * nrow, count), F32),
            pltpu.VMEM((rows, count), BF16),
            pltpu.VMEM((rows, count), BF16),
            pltpu.VMEM((8, count), F32),
            pltpu.VMEM((8, count), F32),
            pltpu.VMEM((blocks, 8, pts), F32),
            pltpu.VMEM((n_gy, own_blocks, 8, pts), F32),
            dma((4,)),
            dma((tiles,)),
            dma((group,)), dma((group,)),
            dma((tiles,)), dma((tiles,)),
            dma((2, tiles)), dma((2, tiles)),
            dma((2,)), dma((2,)),
            dma((2,)),
            dma((n_gy,)), dma((n_gy,)),
        ],
        compiler_params=pltpu.CompilerParams(
            collective_id=0, has_side_effects=True, vmem_limit_bytes=44 * 2**20
        ),
        name="evolve",
    )(
        *(
            pltpu.with_memory_space_constraint(arg, pltpu.HBM)
            for arg in (
                velocity, blade_pos.transpose(1, 0, 2), block_turbine, blade_vel.transpose(1, 0, 2), lift_coeff,
            )
        )
    )
    new, forces = pl.pallas_call(
        write_out,
        out_shape=(jax.ShapeDtypeStruct(velocity.shape, F32), jax.ShapeDtypeStruct(by_comp, F32)),
        in_specs=[vmem, vmem],
        out_specs=(pl.BlockSpec(memory_space=pl.ANY), pl.BlockSpec(memory_space=pl.ANY)),
        scratch_shapes=[dma((comps + 1,))],
        compiler_params=pltpu.CompilerParams(vmem_limit_bytes=16 * 2**20),
        name="write_out",
    )(*made)
    return new, forces.transpose(1, 0, 2)


def solution(mesh):
    sizes = tuple(mesh.shape[axis] for axis in ("gx", "gy", "gz"))
    in_specs = (
        P(None, "gz", "gx", "gy"),
        P(("gx", "gy", "gz"), None, None),
        P(("gx", "gy", "gz")),
        P(("gx", "gy", "gz"), None, None),
        P(("gx", "gy", "gz"), None),
    )
    out_specs = (P(None, "gz", "gx", "gy"), P(("gx", "gy", "gz"), None, None))
    return jax.shard_map(
        functools.partial(local, sizes), mesh=mesh, in_specs=in_specs, out_specs=out_specs, check_vma=False
    )
```

```python
import functools
import math

import jax
import jax.numpy as jnp
from jax import lax
from jax.experimental import pallas as pl
from jax.experimental.pallas import tpu as pltpu
from jax.sharding import PartitionSpec as P

mean_wind = 1.0
viscosity = 0.2
smag_coeff = 0.17
time_step = 0.2
smear = 2.0
smear_norm = 1.0 / (smear**3 * math.pi**1.5)

F32, BF16 = jnp.float32, jnp.bfloat16
MESH = pl.DeviceIdType.MESH
LANES = 128
TOP = 8


def split(value):
    high = value.astype(BF16)
    return high, (value - high.astype(F32)).astype(BF16)


def gaussian(start, count, centers):
    cells = (lax.broadcasted_iota(jnp.int32, (count, 1), 0) + start).astype(F32)
    gap = cells - centers
    return jnp.exp(gap * gap * (-1.0 / (smear * smear)))


def spanwise(win, yd, yl, tile):
    depth = win.shape[2] - 4
    lane = lax.broadcasted_iota(jnp.int32, (16, LANES), 1)
    for z in range(depth):
        for c in range(3):
            left, u, right = (win[tile + side, c, z + 2, TOP : TOP + 16, :] for side in range(3))
            p1 = pltpu.roll(jnp.where(lane < 1, right, u), LANES - 1, 1)
            p2 = pltpu.roll(jnp.where(lane < 2, right, u), LANES - 2, 1)
            m1 = pltpu.roll(jnp.where(lane >= LANES - 1, left, u), 1, 1)
            m2 = pltpu.roll(jnp.where(lane >= LANES - 2, left, u), 2, 1)
            yd[tile, z, c] = 8.0 * (p1 - m1) - (p2 - m2)
            yl[tile, z, c] = 16.0 * (p1 + m1) - (p2 + m2) - 90.0 * u


def stencil(win, yd, yl, tile, z, body):
    grads, laps, own = [], [], []
    for c in range(3):
        def rows(offset, level=0, c=c):
            return win[tile + 1, c, z + 2 + level, TOP + offset : TOP + offset + 16, :]

        u = rows(0)
        x_p1, x_m1, x_p2, x_m2 = rows(1), rows(-1), rows(2), rows(-2)
        z_p1, z_m1, z_p2, z_m2 = rows(0, 1), rows(0, -1), rows(0, 2), rows(0, -2)
        grads.append([8.0 * (x_p1 - x_m1) - (x_p2 - x_m2), yd[tile, z, c], 8.0 * (z_p1 - z_m1) - (z_p2 - z_m2)])
        near = (x_p1 + x_m1) + (z_p1 + z_m1)
        far = (x_p2 + x_m2) + (z_p2 + z_m2)
        laps.append((16.0 * near - far) + yl[tile, z, c])
        own.append(u)
    diag = grads[0][0] * grads[0][0] + grads[1][1] * grads[1][1] + grads[2][2] * grads[2][2]
    both = [grads[i][j] + grads[j][i] for i, j in ((0, 1), (0, 2), (1, 2))]
    cross = both[0] * both[0] + both[1] * both[1] + both[2] * both[2]
    strain = (diag + diag) + cross
    nu = viscosity * time_step / 12.0 + (smag_coeff * smag_coeff * time_step / 144.0) * jnp.sqrt(strain)
    return [
        own[c] + (-mean_wind * time_step / 12.0) * grads[c][0] + nu * laps[c] + time_step * body[c] for c in range(3)
    ]


def kernel(
    sizes, v, pos_in, turb_in, bvel_in, lift_in, out, pf,
    pos, turb, bvel, lift,
    win, vhi, vlo, yd, yl, table, whi, wlo, along, plane, ghi, glo, part, other, back, owned,
    small_sem, load_sem, tab_send, tab_recv, z_send, z_recv, x_send, x_recv, y_send, y_recv,
    part_sem, back_send, back_recv,
):
    n_gx, n_gy, n_gz = sizes
    gx, gy, gz = lax.axis_index("gx"), lax.axis_index("gy"), lax.axis_index("gz")
    mine = gy * n_gz + gz
    group = n_gy * n_gz
    _, depth, nrow, ncol = v.shape
    tiles = ncol // LANES
    own_blocks = pos.shape[1]
    blocks = group * own_blocks
    per_turbine = blocks // n_gy
    pts = pos.shape[2]
    count = per_turbine * pts
    rows = 3 * depth * nrow

    small = [
        pltpu.make_async_copy(src, dst, small_sem.at[i])
        for i, (src, dst) in enumerate(((turb_in, turb), (pos_in, pos), (bvel_in, bvel), (lift_in, lift)))
    ]
    for copy in small:
        copy.start()

    barrier = pltpu.get_barrier_semaphore()
    for step in range(1, group):
        peer = lax.rem(mine + step, group)
        pl.semaphore_signal(
            barrier, 1, device_id={"gy": peer // n_gz, "gz": lax.rem(peer, n_gz)}, device_id_type=MESH
        )

    @pl.when(gx > 0)
    def _():
        pl.semaphore_signal(barrier, 1, device_id={"gx": gx - 1}, device_id_type=MESH)

    @pl.when(gx < n_gx - 1)
    def _():
        pl.semaphore_signal(barrier, 1, device_id={"gx": gx + 1}, device_id_type=MESH)

    def lanes(t):
        return pl.ds(pl.multiple_of(t * LANES, LANES), LANES)

    def load(t):
        return pltpu.make_async_copy(
            v.at[:, :, :, lanes(t)], win.at[t + 1, :, pl.ds(2, depth), pl.ds(TOP, nrow), :], load_sem.at[t]
        )

    @pl.loop(0, tiles)
    def _(t):
        load(t).start()

    for copy in small:
        copy.wait()
    for b in range(own_blocks):
        at = mine * own_blocks + b
        for c in range(3):
            table[at, c : c + 1, :] = pos[c, b : b + 1, :]
            table[at, 3 + c : 4 + c, :] = bvel[c, b : b + 1, :]
        table[at, 6:7, :] = lift[b : b + 1, :]
        table[at, 7:8, :] = jnp.full((1, pts), turb[b].astype(F32))

    z_gap = jnp.where(gz == 0, 0, depth + 2)

    @pl.loop(0, tiles)
    def _(t):
        for c in range(3):
            for k in range(2):
                win[t + 1, c, z_gap + k, TOP : TOP + nrow, :] = jnp.zeros((nrow, LANES), F32)

    @pl.when(gx == 0)
    def _():
        @pl.loop(0, tiles)
        def _(t):
            win[t + 1, :, 2 : 2 + depth, TOP - 2 : TOP, :] = jnp.zeros((3, depth, 2, LANES), F32)

    @pl.when(gx == n_gx - 1)
    def _():
        @pl.loop(0, tiles)
        def _(t):
            win[t + 1, :, 2 : 2 + depth, TOP + nrow : TOP + nrow + 2, :] = jnp.zeros((3, depth, 2, LANES), F32)

    @pl.when(gy == 0)
    def _():
        win[0, :, 2 : 2 + depth, TOP : TOP + nrow, :] = jnp.zeros((3, depth, nrow, LANES), F32)

    @pl.when(gy == n_gy - 1)
    def _():
        win[tiles + 1, :, 2 : 2 + depth, TOP : TOP + nrow, :] = jnp.zeros((3, depth, nrow, LANES), F32)

    pl.semaphore_wait(barrier, group - 1 + (gx > 0).astype(jnp.int32) + (gx < n_gx - 1).astype(jnp.int32))

    def remote(src, dst, send, recv, device):
        return pltpu.make_async_remote_copy(
            src_ref=src, dst_ref=dst, send_sem=send, recv_sem=recv, device_id=device, device_id_type=MESH
        )

    own_slots = pl.ds(mine * own_blocks, own_blocks)

    def tab(step):
        peer = lax.rem(mine + step, group)
        return remote(
            table.at[own_slots], table.at[own_slots], tab_send.at[step], tab_recv.at[step],
            {"gy": peer // n_gz, "gz": lax.rem(peer, n_gz)},
        )

    z_from = jnp.where(gz == 0, depth - 2, 0)
    z_to = jnp.where(gz == 0, 0, depth + 2)

    def z_copy(t):
        return remote(
            v.at[:, pl.ds(z_from, 2), :, lanes(t)],
            win.at[t + 1, :, pl.ds(z_to, 2), pl.ds(TOP, nrow), :],
            z_send.at[t], z_recv.at[t], {"gz": 1 - gz},
        )

    def x_up(t):
        return remote(
            v.at[:, :, pl.ds(nrow - 2, 2), lanes(t)],
            win.at[t + 1, :, pl.ds(2, depth), pl.ds(TOP - 2, 2), :],
            x_send.at[0, t], x_recv.at[0, t], {"gx": gx + 1},
        )

    def x_down(t):
        return remote(
            v.at[:, :, pl.ds(0, 2), lanes(t)],
            win.at[t + 1, :, pl.ds(2, depth), pl.ds(TOP + nrow, 2), :],
            x_send.at[1, t], x_recv.at[1, t], {"gx": gx - 1},
        )

    def y_copy(side):
        first = 0 if side else ncol - LANES
        return remote(
            v.at[:, :, :, pl.ds(first, LANES)],
            win.at[tiles + 1 if side else 0, :, pl.ds(2, depth), pl.ds(TOP, nrow), :],
            y_send.at[side], y_recv.at[side], {"gy": gy - 1 if side else gy + 1},
        )

    for step in range(1, group):
        tab(step).start()

    @pl.when(gy > 0)
    def _():
        y_copy(1).start()

    @pl.when(gy < n_gy - 1)
    def _():
        y_copy(0).start()

    @pl.loop(0, tiles)
    def _(t):
        @pl.when(gx < n_gx - 1)
        def _():
            x_up(t).start()

        @pl.when(gx > 0)
        def _():
            x_down(t).start()

        z_copy(t).start()

    @pl.loop(0, tiles)
    def _(t):
        load(t).wait()
        high, low = split(win[t + 1, :, 2 : 2 + depth, TOP : TOP + nrow, :].reshape(rows, LANES))
        vhi[t] = high
        vlo[t] = low

    for step in range(1, group):
        tab(step).wait_recv()
    turbine = gy.astype(F32)

    def matches():
        rank = jnp.zeros((8, pts), F32)
        for s in range(blocks):
            entry = table[s]
            match = jnp.broadcast_to(entry[7:8, :], (8, pts)) == turbine
            yield s, entry, [match & (rank == float(k)) for k in range(per_turbine)]
            rank = rank + jnp.where(match, 1.0, 0.0)

    slots = [jnp.zeros((8, pts), F32) for _ in range(per_turbine)]
    for _, entry, chosen in matches():
        slots = [jnp.where(one, entry, held) for one, held in zip(chosen, slots)]

    def flat(row):
        return jnp.concatenate([slot[row : row + 1, :] for slot in slots], axis=1)

    weight_x = gaussian(gx * nrow, nrow, flat(0))
    weight_z = gaussian(gz * depth, depth, flat(2))
    for z in range(depth):
        plane[z * nrow : (z + 1) * nrow, :] = weight_z[z : z + 1, :] * weight_x
    center_y = flat(1)

    per_step = 4
    step_cols = per_step * LANES
    steps = ncol // step_cols

    for j in range(steps):
        at = j * step_cols
        high, low = split(gaussian(gy * ncol + at, step_cols, center_y))
        whi[at : at + step_cols, :] = high
        wlo[at : at + step_cols, :] = low
        vh, vl = (
            jnp.concatenate([term[per_step * j + k] for k in range(per_step)], axis=1) for term in (vhi, vlo)
        )
        dot = functools.partial(jnp.dot, preferred_element_type=F32)
        now = dot(jnp.concatenate([vh, vl], axis=1), jnp.concatenate([high, high], axis=0)) + dot(vh, low)
        if j == 0:
            along[...] = now
        else:
            along[...] += now

    per_comp = depth * nrow
    part[3:8, :] = jnp.zeros((5, count), F32)
    for c in range(3):
        part[c : c + 1, :] = jnp.sum(
            along[c * per_comp : (c + 1) * per_comp, :] * plane[...], axis=0, keepdims=True
        )
    swap = remote(part, other, part_sem.at[0], part_sem.at[1], {"gz": 1 - gz})
    swap.start()
    swap.wait_recv()
    relative = [
        smear_norm * (part[c : c + 1, :] + other[c : c + 1, :]) - flat(3 + c) for c in range(3)
    ]
    speed = jnp.sqrt(relative[0] * relative[0] + relative[1] * relative[1] + relative[2] * relative[2])
    force = [-flat(6) * speed * relative[c] for c in range(3)]

    stacked = [
        jnp.concatenate(
            [force[c][:, k * pts : (k + 1) * pts] for c in range(3)] + [jnp.zeros((5, pts), F32)], axis=0
        )
        for k in range(per_turbine)
    ]
    for s, _, chosen in matches():
        back[s] = sum(jnp.where(one, held, 0.0) for one, held in zip(chosen, stacked))

    def give(step):
        peer = lax.rem(gy + step, n_gy)
        return remote(
            back.at[pl.ds((peer * n_gz + gz) * own_blocks, own_blocks)], owned.at[step],
            back_send.at[step], back_recv.at[step], {"gy": peer},
        )

    for step in range(1, n_gy):
        give(step).start()

    for c in range(3):
        high, low = split((smear_norm * force[c]) * plane[...])
        ghi[c * per_comp : (c + 1) * per_comp, :] = high
        glo[c * per_comp : (c + 1) * per_comp, :] = low

    @pl.when(gy > 0)
    def _():
        y_copy(0).wait_recv()

    @pl.when(gy < n_gy - 1)
    def _():
        y_copy(1).wait_recv()

    @pl.loop(0, steps)
    def _(j):
        at = pl.multiple_of(j * step_cols, step_cols)
        high, low = whi[pl.ds(at, step_cols), :], wlo[pl.ds(at, step_cols), :]

        def dot(a, b):
            return lax.dot_general(a, b, (((1,), (1,)), ((), ())), preferred_element_type=F32)

        both = jnp.concatenate([ghi[...], glo[...]], axis=1)
        along[...] = dot(both, jnp.concatenate([high, high], axis=1)) + dot(ghi[...], low)
        for k in range(per_step):
            spanwise(win, yd, yl, per_step * j + k)

        @pl.loop(0, per_step)
        def _(k):
            t = per_step * j + k

            @pl.when(gx > 0)
            def _():
                x_up(t).wait_recv()

            @pl.when(gx < n_gx - 1)
            def _():
                x_down(t).wait_recv()

            z_copy(t).wait_recv()
            for z in range(depth):
                body = [
                    along[c * per_comp + z * nrow : c * per_comp + (z + 1) * nrow, lanes(k)]
                    for c in range(3)
                ]
                new = stencil(win, yd, yl, t, z, body)
                for c in range(3):
                    out[c, z, :, lanes(t)] = new[c]

    for step in range(1, n_gy):
        give(step).wait()
    total = back[own_slots] + sum(owned[step] for step in range(1, n_gy))
    for c in range(3):
        for b in range(own_blocks):
            pf[c, b : b + 1, :] = total[b, c : c + 1, :]
    for step in range(1, group):
        tab(step).wait_send()
    swap.wait_send()

    @pl.when(gy > 0)
    def _():
        y_copy(1).wait_send()

    @pl.when(gy < n_gy - 1)
    def _():
        y_copy(0).wait_send()

    @pl.loop(0, tiles)
    def _(t):
        @pl.when(gx < n_gx - 1)
        def _():
            x_up(t).wait_send()

        @pl.when(gx > 0)
        def _():
            x_down(t).wait_send()

        z_copy(t).wait_send()


def write_out(new, forces, new_out, forces_out, sem):
    copies = [pltpu.make_async_copy(forces, forces_out, sem.at[0])]
    for c in range(new.shape[0]):
        copies.append(pltpu.make_async_copy(new.at[c], new_out.at[c], sem.at[c + 1]))
    for copy in copies:
        copy.start()
    for copy in copies:
        copy.wait()


def local(sizes, velocity, blade_pos, block_turbine, blade_vel, lift_coeff):
    n_gx, n_gy, n_gz = sizes
    comps, depth, nrow, ncol = velocity.shape
    own_blocks, _, pts = blade_pos.shape
    tiles = ncol // LANES
    group = n_gy * n_gz
    blocks = group * own_blocks
    count = blocks // n_gy * pts
    rows = comps * depth * nrow
    dma = pltpu.SemaphoreType.DMA
    vmem = pl.BlockSpec(memory_space=pltpu.VMEM)
    by_comp = (blade_pos.shape[1], own_blocks, pts)
    made = pl.pallas_call(
        functools.partial(kernel, sizes),
        out_shape=(pltpu.VMEM(velocity.shape, F32), pltpu.VMEM(by_comp, F32)),
        in_specs=[pl.BlockSpec(memory_space=pl.ANY)] * 5,
        out_specs=(vmem, vmem),
        scratch_shapes=[
            pltpu.VMEM(by_comp, F32),
            pltpu.SMEM((own_blocks,), jnp.int32),
            pltpu.VMEM(by_comp, F32),
            pltpu.VMEM((own_blocks, pts), F32),
            pltpu.VMEM((tiles + 2, comps, depth + 4, nrow + 16, LANES), F32),
            pltpu.VMEM((tiles, rows, LANES), BF16),
            pltpu.VMEM((tiles, rows, LANES), BF16),
            pltpu.VMEM((tiles, depth, comps, nrow, LANES), F32),
            pltpu.VMEM((tiles, depth, comps, nrow, LANES), F32),
            pltpu.VMEM((blocks, 8, pts), F32),
            pltpu.VMEM((ncol, count), BF16),
            pltpu.VMEM((ncol, count), BF16),
            pltpu.VMEM((rows, count), F32),
            pltpu.VMEM((depth * nrow, count), F32),
            pltpu.VMEM((rows, count), BF16),
            pltpu.VMEM((rows, count), BF16),
            pltpu.VMEM((8, count), F32),
            pltpu.VMEM((8, count), F32),
            pltpu.VMEM((blocks, 8, pts), F32),
            pltpu.VMEM((n_gy, own_blocks, 8, pts), F32),
            dma((4,)),
            dma((tiles,)),
            dma((group,)), dma((group,)),
            dma((tiles,)), dma((tiles,)),
            dma((2, tiles)), dma((2, tiles)),
            dma((2,)), dma((2,)),
            dma((2,)),
            dma((n_gy,)), dma((n_gy,)),
        ],
        compiler_params=pltpu.CompilerParams(
            collective_id=0, has_side_effects=True, vmem_limit_bytes=54 * 2**20
        ),
        name="evolve",
    )(
        *(
            pltpu.with_memory_space_constraint(arg, pltpu.HBM)
            for arg in (
                velocity, blade_pos.transpose(1, 0, 2), block_turbine, blade_vel.transpose(1, 0, 2), lift_coeff,
            )
        )
    )
    new, forces = pl.pallas_call(
        write_out,
        out_shape=(jax.ShapeDtypeStruct(velocity.shape, F32), jax.ShapeDtypeStruct(by_comp, F32)),
        in_specs=[vmem, vmem],
        out_specs=(pl.BlockSpec(memory_space=pl.ANY), pl.BlockSpec(memory_space=pl.ANY)),
        scratch_shapes=[dma((comps + 1,))],
        compiler_params=pltpu.CompilerParams(vmem_limit_bytes=16 * 2**20),
        name="write_out",
    )(*made)
    return new, forces.transpose(1, 0, 2)


def solution(mesh):
    sizes = tuple(mesh.shape[axis] for axis in ("gx", "gy", "gz"))
    in_specs = (
        P(None, "gz", "gx", "gy"),
        P(("gx", "gy", "gz"), None, None),
        P(("gx", "gy", "gz")),
        P(("gx", "gy", "gz"), None, None),
        P(("gx", "gy", "gz"), None),
    )
    out_specs = (P(None, "gz", "gx", "gy"), P(("gx", "gy", "gz"), None, None))
    return jax.shard_map(
        functools.partial(local, sizes), mesh=mesh, in_specs=in_specs, out_specs=out_specs, check_vma=False
    )
```

```python
import functools
import math

import jax
import jax.numpy as jnp
from jax import lax
from jax.experimental import pallas as pl
from jax.experimental.pallas import tpu as pltpu
from jax.sharding import PartitionSpec as P

mean_wind = 1.0
viscosity = 0.2
smag_coeff = 0.17
time_step = 0.2
smear = 2.0
smear_norm = 1.0 / (smear**3 * math.pi**1.5)

F32, BF16 = jnp.float32, jnp.bfloat16
MESH = pl.DeviceIdType.MESH
LANES = 128
TINY = float(jnp.finfo(F32).tiny)
TOP = 8


def split(value):
    high = value.astype(BF16)
    return high, (value - high.astype(F32)).astype(BF16)


def gaussian(start, count, centers):
    cells = (lax.broadcasted_iota(jnp.int32, (count, 1), 0) + start).astype(F32)
    gap = cells - centers
    return jnp.exp(gap * gap * (-1.0 / (smear * smear)))


def spanwise(win, yd, yl, tile):
    depth = win.shape[2] - 4
    lane = lax.broadcasted_iota(jnp.int32, (16, LANES), 1)
    for z in range(depth):
        for c in range(3):
            left, u, right = (win[tile + side, c, z + 2, TOP : TOP + 16, :] for side in range(3))
            p1 = pltpu.roll(jnp.where(lane < 1, right, u), LANES - 1, 1)
            p2 = pltpu.roll(jnp.where(lane < 2, right, u), LANES - 2, 1)
            m1 = pltpu.roll(jnp.where(lane >= LANES - 1, left, u), 1, 1)
            m2 = pltpu.roll(jnp.where(lane >= LANES - 2, left, u), 2, 1)
            yd[tile, z, c] = 8.0 * (p1 - m1) - (p2 - m2)
            yl[tile, z, c] = 16.0 * (p1 + m1) - (p2 + m2) - 90.0 * u


def stencil(win, yd, yl, tile, z, body):
    grads, laps, own = [], [], []
    for c in range(3):
        def rows(offset, level=0, c=c):
            return win[tile + 1, c, z + 2 + level, TOP + offset : TOP + offset + 16, :]

        u = rows(0)
        x_p1, x_m1, x_p2, x_m2 = rows(1), rows(-1), rows(2), rows(-2)
        z_p1, z_m1, z_p2, z_m2 = rows(0, 1), rows(0, -1), rows(0, 2), rows(0, -2)
        grads.append([8.0 * (x_p1 - x_m1) - (x_p2 - x_m2), yd[tile, z, c], 8.0 * (z_p1 - z_m1) - (z_p2 - z_m2)])
        near = (x_p1 + x_m1) + (z_p1 + z_m1)
        far = (x_p2 + x_m2) + (z_p2 + z_m2)
        laps.append((16.0 * near - far) + yl[tile, z, c])
        own.append(u)
    diag = grads[0][0] * grads[0][0] + grads[1][1] * grads[1][1] + grads[2][2] * grads[2][2]
    both = [grads[i][j] + grads[j][i] for i, j in ((0, 1), (0, 2), (1, 2))]
    cross = both[0] * both[0] + both[1] * both[1] + both[2] * both[2]
    strain = (diag + diag) + cross
    nu = viscosity * time_step / 12.0 + (smag_coeff * smag_coeff * time_step / 144.0) * (
        strain * lax.rsqrt(jnp.maximum(strain, TINY))
    )
    return [
        own[c] + (-mean_wind * time_step / 12.0) * grads[c][0] + nu * laps[c] + body[c] for c in range(3)
    ]


def kernel(
    sizes, v, pos_in, turb_in, bvel_in, lift_in, out, pf,
    pos, turb, bvel, lift,
    win, vhi, vlo, yd, yl, table, whi, wlo, along, plane, ghi, glo, part, other, back, owned,
    small_sem, load_sem, tab_send, tab_recv, z_send, z_recv, x_send, x_recv, y_send, y_recv,
    part_sem, back_send, back_recv,
):
    n_gx, n_gy, n_gz = sizes
    gx, gy, gz = lax.axis_index("gx"), lax.axis_index("gy"), lax.axis_index("gz")
    mine = gy * n_gz + gz
    group = n_gy * n_gz
    _, depth, nrow, ncol = v.shape
    tiles = ncol // LANES
    own_blocks = pos.shape[1]
    blocks = group * own_blocks
    per_turbine = blocks // n_gy
    pts = pos.shape[2]
    count = per_turbine * pts
    rows = 3 * depth * nrow

    small = [
        pltpu.make_async_copy(src, dst, small_sem.at[i])
        for i, (src, dst) in enumerate(((turb_in, turb), (pos_in, pos), (bvel_in, bvel), (lift_in, lift)))
    ]
    for copy in small:
        copy.start()

    barrier = pltpu.get_barrier_semaphore()
    for step in range(1, group):
        peer = lax.rem(mine + step, group)
        pl.semaphore_signal(
            barrier, 1, device_id={"gy": peer // n_gz, "gz": lax.rem(peer, n_gz)}, device_id_type=MESH
        )

    @pl.when(gx > 0)
    def _():
        pl.semaphore_signal(barrier, 1, device_id={"gx": gx - 1}, device_id_type=MESH)

    @pl.when(gx < n_gx - 1)
    def _():
        pl.semaphore_signal(barrier, 1, device_id={"gx": gx + 1}, device_id_type=MESH)

    def lanes(t):
        return pl.ds(pl.multiple_of(t * LANES, LANES), LANES)

    def load(t):
        return pltpu.make_async_copy(
            v.at[:, :, :, lanes(t)], win.at[t + 1, :, pl.ds(2, depth), pl.ds(TOP, nrow), :], load_sem.at[t]
        )

    @pl.loop(0, tiles)
    def _(t):
        load(t).start()

    for copy in small:
        copy.wait()
    for b in range(own_blocks):
        at = mine * own_blocks + b
        for c in range(3):
            table[at, c : c + 1, :] = pos[c, b : b + 1, :]
            table[at, 3 + c : 4 + c, :] = bvel[c, b : b + 1, :]
        table[at, 6:7, :] = lift[b : b + 1, :]
        table[at, 7:8, :] = jnp.full((1, pts), turb[b].astype(F32))

    z_gap = jnp.where(gz == 0, 0, depth + 2)

    @pl.loop(0, tiles)
    def _(t):
        for c in range(3):
            for k in range(2):
                win[t + 1, c, z_gap + k, TOP : TOP + nrow, :] = jnp.zeros((nrow, LANES), F32)

    @pl.when(gx == 0)
    def _():
        @pl.loop(0, tiles)
        def _(t):
            win[t + 1, :, 2 : 2 + depth, TOP - 2 : TOP, :] = jnp.zeros((3, depth, 2, LANES), F32)

    @pl.when(gx == n_gx - 1)
    def _():
        @pl.loop(0, tiles)
        def _(t):
            win[t + 1, :, 2 : 2 + depth, TOP + nrow : TOP + nrow + 2, :] = jnp.zeros((3, depth, 2, LANES), F32)

    @pl.when(gy == 0)
    def _():
        win[0, :, 2 : 2 + depth, TOP : TOP + nrow, :] = jnp.zeros((3, depth, nrow, LANES), F32)

    @pl.when(gy == n_gy - 1)
    def _():
        win[tiles + 1, :, 2 : 2 + depth, TOP : TOP + nrow, :] = jnp.zeros((3, depth, nrow, LANES), F32)

    pl.semaphore_wait(barrier, group - 1 + (gx > 0).astype(jnp.int32) + (gx < n_gx - 1).astype(jnp.int32))

    def remote(src, dst, send, recv, device):
        return pltpu.make_async_remote_copy(
            src_ref=src, dst_ref=dst, send_sem=send, recv_sem=recv, device_id=device, device_id_type=MESH
        )

    own_slots = pl.ds(mine * own_blocks, own_blocks)

    def tab(step):
        peer = lax.rem(mine + step, group)
        return remote(
            table.at[own_slots], table.at[own_slots], tab_send.at[step], tab_recv.at[step],
            {"gy": peer // n_gz, "gz": lax.rem(peer, n_gz)},
        )

    z_from = jnp.where(gz == 0, depth - 2, 0)
    z_to = jnp.where(gz == 0, 0, depth + 2)

    def z_copy(t):
        return remote(
            v.at[:, pl.ds(z_from, 2), :, lanes(t)],
            win.at[t + 1, :, pl.ds(z_to, 2), pl.ds(TOP, nrow), :],
            z_send.at[t], z_recv.at[t], {"gz": 1 - gz},
        )

    def x_up(t):
        return remote(
            v.at[:, :, pl.ds(nrow - 2, 2), lanes(t)],
            win.at[t + 1, :, pl.ds(2, depth), pl.ds(TOP - 2, 2), :],
            x_send.at[0, t], x_recv.at[0, t], {"gx": gx + 1},
        )

    def x_down(t):
        return remote(
            v.at[:, :, pl.ds(0, 2), lanes(t)],
            win.at[t + 1, :, pl.ds(2, depth), pl.ds(TOP + nrow, 2), :],
            x_send.at[1, t], x_recv.at[1, t], {"gx": gx - 1},
        )

    def y_copy(side):
        first = 0 if side else ncol - LANES
        return remote(
            v.at[:, :, :, pl.ds(first, LANES)],
            win.at[tiles + 1 if side else 0, :, pl.ds(2, depth), pl.ds(TOP, nrow), :],
            y_send.at[side], y_recv.at[side], {"gy": gy - 1 if side else gy + 1},
        )

    for step in range(1, group):
        tab(step).start()

    @pl.when(gy > 0)
    def _():
        y_copy(1).start()

    @pl.when(gy < n_gy - 1)
    def _():
        y_copy(0).start()

    @pl.loop(0, tiles)
    def _(t):
        @pl.when(gx < n_gx - 1)
        def _():
            x_up(t).start()

        @pl.when(gx > 0)
        def _():
            x_down(t).start()

        z_copy(t).start()

    @pl.loop(0, tiles)
    def _(t):
        load(t).wait()
        high, low = split(win[t + 1, :, 2 : 2 + depth, TOP : TOP + nrow, :].reshape(rows, LANES))
        vhi[t] = high
        vlo[t] = low

    for step in range(1, group):
        tab(step).wait_recv()
    turbine = gy.astype(F32)

    def matches():
        rank = jnp.zeros((8, pts), F32)
        for s in range(blocks):
            entry = table[s]
            match = jnp.broadcast_to(entry[7:8, :], (8, pts)) == turbine
            yield s, entry, [match & (rank == float(k)) for k in range(per_turbine)]
            rank = rank + jnp.where(match, 1.0, 0.0)

    slots = [jnp.zeros((8, pts), F32) for _ in range(per_turbine)]
    for _, entry, chosen in matches():
        slots = [jnp.where(one, entry, held) for one, held in zip(chosen, slots)]

    def flat(row):
        return jnp.concatenate([slot[row : row + 1, :] for slot in slots], axis=1)

    weight_x = gaussian(gx * nrow, nrow, flat(0))
    weight_z = gaussian(gz * depth, depth, flat(2))
    for z in range(depth):
        plane[z * nrow : (z + 1) * nrow, :] = weight_z[z : z + 1, :] * weight_x
    center_y = flat(1)

    per_step = 4
    step_cols = per_step * LANES
    steps = ncol // step_cols

    for j in range(steps):
        at = j * step_cols
        high, low = split(gaussian(gy * ncol + at, step_cols, center_y))
        whi[at : at + step_cols, :] = high
        wlo[at : at + step_cols, :] = low
        vh, vl = (
            jnp.concatenate([term[per_step * j + k] for k in range(per_step)], axis=1) for term in (vhi, vlo)
        )
        dot = functools.partial(jnp.dot, preferred_element_type=F32)
        now = dot(jnp.concatenate([vh, vl], axis=1), jnp.concatenate([high, high], axis=0)) + dot(vh, low)
        if j == 0:
            along[...] = now
        else:
            along[...] += now

    per_comp = depth * nrow
    part[3:8, :] = jnp.zeros((5, count), F32)
    for c in range(3):
        part[c : c + 1, :] = jnp.sum(
            along[c * per_comp : (c + 1) * per_comp, :] * plane[...], axis=0, keepdims=True
        )
    swap = remote(part, other, part_sem.at[0], part_sem.at[1], {"gz": 1 - gz})
    swap.start()
    swap.wait_recv()
    relative = [
        smear_norm * (part[c : c + 1, :] + other[c : c + 1, :]) - flat(3 + c) for c in range(3)
    ]
    speed = jnp.sqrt(relative[0] * relative[0] + relative[1] * relative[1] + relative[2] * relative[2])
    force = [-flat(6) * speed * relative[c] for c in range(3)]

    stacked = [
        jnp.concatenate(
            [force[c][:, k * pts : (k + 1) * pts] for c in range(3)] + [jnp.zeros((5, pts), F32)], axis=0
        )
        for k in range(per_turbine)
    ]
    for s, _, chosen in matches():
        back[s] = sum(jnp.where(one, held, 0.0) for one, held in zip(chosen, stacked))

    def give(step):
        peer = lax.rem(gy + step, n_gy)
        return remote(
            back.at[pl.ds((peer * n_gz + gz) * own_blocks, own_blocks)], owned.at[step],
            back_send.at[step], back_recv.at[step], {"gy": peer},
        )

    for step in range(1, n_gy):
        give(step).start()

    for c in range(3):
        high, low = split((time_step * smear_norm * force[c]) * plane[...])
        ghi[c * per_comp : (c + 1) * per_comp, :] = high
        glo[c * per_comp : (c + 1) * per_comp, :] = low

    @pl.when(gy > 0)
    def _():
        y_copy(0).wait_recv()

    @pl.when(gy < n_gy - 1)
    def _():
        y_copy(1).wait_recv()

    @pl.loop(0, steps)
    def _(j):
        at = pl.multiple_of(j * step_cols, step_cols)
        high, low = whi[pl.ds(at, step_cols), :], wlo[pl.ds(at, step_cols), :]

        def dot(a, b):
            return lax.dot_general(a, b, (((1,), (1,)), ((), ())), preferred_element_type=F32)

        both = jnp.concatenate([ghi[...], glo[...]], axis=1)
        along[...] = dot(both, jnp.concatenate([high, high], axis=1)) + dot(ghi[...], low)
        for k in range(per_step):
            spanwise(win, yd, yl, per_step * j + k)

        @pl.loop(0, per_step)
        def _(k):
            t = per_step * j + k

            @pl.when(gx > 0)
            def _():
                x_up(t).wait_recv()

            @pl.when(gx < n_gx - 1)
            def _():
                x_down(t).wait_recv()

            z_copy(t).wait_recv()
            for z in range(depth):
                body = [
                    along[c * per_comp + z * nrow : c * per_comp + (z + 1) * nrow, lanes(k)]
                    for c in range(3)
                ]
                new = stencil(win, yd, yl, t, z, body)
                for c in range(3):
                    out[c, z, :, lanes(t)] = new[c]

    for step in range(1, n_gy):
        give(step).wait()
    total = back[own_slots] + sum(owned[step] for step in range(1, n_gy))
    for c in range(3):
        for b in range(own_blocks):
            pf[c, b : b + 1, :] = total[b, c : c + 1, :]
    for step in range(1, group):
        tab(step).wait_send()
    swap.wait_send()

    @pl.when(gy > 0)
    def _():
        y_copy(1).wait_send()

    @pl.when(gy < n_gy - 1)
    def _():
        y_copy(0).wait_send()

    @pl.loop(0, tiles)
    def _(t):
        @pl.when(gx < n_gx - 1)
        def _():
            x_up(t).wait_send()

        @pl.when(gx > 0)
        def _():
            x_down(t).wait_send()

        z_copy(t).wait_send()


def write_out(new, forces, new_out, forces_out, sem):
    copies = [pltpu.make_async_copy(forces, forces_out, sem.at[0])]
    for c in range(new.shape[0]):
        copies.append(pltpu.make_async_copy(new.at[c], new_out.at[c], sem.at[c + 1]))
    for copy in copies:
        copy.start()
    for copy in copies:
        copy.wait()


def local(sizes, velocity, blade_pos, block_turbine, blade_vel, lift_coeff):
    n_gx, n_gy, n_gz = sizes
    comps, depth, nrow, ncol = velocity.shape
    own_blocks, _, pts = blade_pos.shape
    tiles = ncol // LANES
    group = n_gy * n_gz
    blocks = group * own_blocks
    count = blocks // n_gy * pts
    rows = comps * depth * nrow
    dma = pltpu.SemaphoreType.DMA
    vmem = pl.BlockSpec(memory_space=pltpu.VMEM)
    by_comp = (blade_pos.shape[1], own_blocks, pts)
    made = pl.pallas_call(
        functools.partial(kernel, sizes),
        out_shape=(pltpu.VMEM(velocity.shape, F32), pltpu.VMEM(by_comp, F32)),
        in_specs=[pl.BlockSpec(memory_space=pl.ANY)] * 5,
        out_specs=(vmem, vmem),
        scratch_shapes=[
            pltpu.VMEM(by_comp, F32),
            pltpu.SMEM((own_blocks,), jnp.int32),
            pltpu.VMEM(by_comp, F32),
            pltpu.VMEM((own_blocks, pts), F32),
            pltpu.VMEM((tiles + 2, comps, depth + 4, nrow + 16, LANES), F32),
            pltpu.VMEM((tiles, rows, LANES), BF16),
            pltpu.VMEM((tiles, rows, LANES), BF16),
            pltpu.VMEM((tiles, depth, comps, nrow, LANES), F32),
            pltpu.VMEM((tiles, depth, comps, nrow, LANES), F32),
            pltpu.VMEM((blocks, 8, pts), F32),
            pltpu.VMEM((ncol, count), BF16),
            pltpu.VMEM((ncol, count), BF16),
            pltpu.VMEM((rows, count), F32),
            pltpu.VMEM((depth * nrow, count), F32),
            pltpu.VMEM((rows, count), BF16),
            pltpu.VMEM((rows, count), BF16),
            pltpu.VMEM((8, count), F32),
            pltpu.VMEM((8, count), F32),
            pltpu.VMEM((blocks, 8, pts), F32),
            pltpu.VMEM((n_gy, own_blocks, 8, pts), F32),
            dma((4,)),
            dma((tiles,)),
            dma((group,)), dma((group,)),
            dma((tiles,)), dma((tiles,)),
            dma((2, tiles)), dma((2, tiles)),
            dma((2,)), dma((2,)),
            dma((2,)),
            dma((n_gy,)), dma((n_gy,)),
        ],
        compiler_params=pltpu.CompilerParams(
            collective_id=0, has_side_effects=True, vmem_limit_bytes=54 * 2**20
        ),
        name="evolve",
    )(
        *(
            pltpu.with_memory_space_constraint(arg, pltpu.HBM)
            for arg in (
                velocity, blade_pos.transpose(1, 0, 2), block_turbine, blade_vel.transpose(1, 0, 2), lift_coeff,
            )
        )
    )
    new, forces = pl.pallas_call(
        write_out,
        out_shape=(jax.ShapeDtypeStruct(velocity.shape, F32), jax.ShapeDtypeStruct(by_comp, F32)),
        in_specs=[vmem, vmem],
        out_specs=(pl.BlockSpec(memory_space=pl.ANY), pl.BlockSpec(memory_space=pl.ANY)),
        scratch_shapes=[dma((comps + 1,))],
        compiler_params=pltpu.CompilerParams(vmem_limit_bytes=16 * 2**20),
        name="write_out",
    )(*made)
    return new, forces.transpose(1, 0, 2)


def solution(mesh):
    sizes = tuple(mesh.shape[axis] for axis in ("gx", "gy", "gz"))
    in_specs = (
        P(None, "gz", "gx", "gy"),
        P(("gx", "gy", "gz"), None, None),
        P(("gx", "gy", "gz")),
        P(("gx", "gy", "gz"), None, None),
        P(("gx", "gy", "gz"), None),
    )
    out_specs = (P(None, "gz", "gx", "gy"), P(("gx", "gy", "gz"), None, None))
    return jax.shard_map(
        functools.partial(local, sizes), mesh=mesh, in_specs=in_specs, out_specs=out_specs, check_vma=False
    )
```

```python
import functools
import math

import jax
import jax.numpy as jnp
from jax import lax
from jax.experimental import pallas as pl
from jax.experimental.pallas import tpu as pltpu
from jax.sharding import PartitionSpec as P

mean_wind = 1.0
viscosity = 0.2
smag_coeff = 0.17
time_step = 0.2
smear = 2.0
smear_norm = 1.0 / (smear**3 * math.pi**1.5)

F32, BF16 = jnp.float32, jnp.bfloat16
MESH = pl.DeviceIdType.MESH
LANES = 128
TINY = float(jnp.finfo(F32).tiny)
TOP = 8


def split(value):
    high = value.astype(BF16)
    return high, (value - high.astype(F32)).astype(BF16)


def gaussian(start, count, centers):
    cells = (lax.broadcasted_iota(jnp.int32, (count, 1), 0) + start).astype(F32)
    gap = cells - centers
    return jnp.exp2(gap * gap * (-math.log2(math.e) / (smear * smear)))


def spanwise(win, yd, yl, tile):
    depth = win.shape[2] - 4
    lane = lax.broadcasted_iota(jnp.int32, (16, LANES), 1)
    for z in range(depth):
        for c in range(3):
            left, u, right = (win[tile + side, c, z + 2, TOP : TOP + 16, :] for side in range(3))
            p1 = pltpu.roll(jnp.where(lane < 1, right, u), LANES - 1, 1)
            p2 = pltpu.roll(jnp.where(lane < 2, right, u), LANES - 2, 1)
            m1 = pltpu.roll(jnp.where(lane >= LANES - 1, left, u), 1, 1)
            m2 = pltpu.roll(jnp.where(lane >= LANES - 2, left, u), 2, 1)
            yd[tile, z, c] = 8.0 * (p1 - m1) - (p2 - m2)
            yl[tile, z, c] = 16.0 * (p1 + m1) - (p2 + m2) - 90.0 * u


def stencil(win, yd, yl, tile, z, body):
    grads, laps, own = [], [], []
    for c in range(3):
        def rows(offset, level=0, c=c):
            return win[tile + 1, c, z + 2 + level, TOP + offset : TOP + offset + 16, :]

        u = rows(0)
        x_p1, x_m1, x_p2, x_m2 = rows(1), rows(-1), rows(2), rows(-2)
        z_p1, z_m1, z_p2, z_m2 = rows(0, 1), rows(0, -1), rows(0, 2), rows(0, -2)
        grads.append([8.0 * (x_p1 - x_m1) - (x_p2 - x_m2), yd[tile, z, c], 8.0 * (z_p1 - z_m1) - (z_p2 - z_m2)])
        near = (x_p1 + x_m1) + (z_p1 + z_m1)
        far = (x_p2 + x_m2) + (z_p2 + z_m2)
        laps.append((16.0 * near - far) + yl[tile, z, c])
        own.append(u)
    diag = grads[0][0] * grads[0][0] + grads[1][1] * grads[1][1] + grads[2][2] * grads[2][2]
    both = [grads[i][j] + grads[j][i] for i, j in ((0, 1), (0, 2), (1, 2))]
    cross = both[0] * both[0] + both[1] * both[1] + both[2] * both[2]
    strain = (diag + diag) + cross
    nu = viscosity * time_step / 12.0 + (smag_coeff * smag_coeff * time_step / 144.0) * (
        strain * lax.rsqrt(jnp.maximum(strain, TINY))
    )
    return [
        own[c] + (-mean_wind * time_step / 12.0) * grads[c][0] + nu * laps[c] + body[c] for c in range(3)
    ]


def kernel(
    sizes, v, pos_in, turb_in, bvel_in, lift_in, out, pf,
    pos, turb, bvel, lift,
    win, vhi, vlo, yd, yl, table, whi, wlo, along, plane, ghi, glo, part, other, back, owned,
    small_sem, load_sem, tab_send, tab_recv, z_send, z_recv, x_send, x_recv, y_send, y_recv,
    part_sem, back_send, back_recv,
):
    n_gx, n_gy, n_gz = sizes
    gx, gy, gz = lax.axis_index("gx"), lax.axis_index("gy"), lax.axis_index("gz")
    mine = gy * n_gz + gz
    group = n_gy * n_gz
    _, depth, nrow, ncol = v.shape
    tiles = ncol // LANES
    own_blocks = pos.shape[1]
    blocks = group * own_blocks
    per_turbine = blocks // n_gy
    pts = pos.shape[2]
    count = per_turbine * pts
    rows = 3 * depth * nrow

    small = [
        pltpu.make_async_copy(src, dst, small_sem.at[i])
        for i, (src, dst) in enumerate(((turb_in, turb), (pos_in, pos), (bvel_in, bvel), (lift_in, lift)))
    ]
    for copy in small:
        copy.start()

    barrier = pltpu.get_barrier_semaphore()
    for step in range(1, group):
        peer = lax.rem(mine + step, group)
        pl.semaphore_signal(
            barrier, 1, device_id={"gy": peer // n_gz, "gz": lax.rem(peer, n_gz)}, device_id_type=MESH
        )

    @pl.when(gx > 0)
    def _():
        pl.semaphore_signal(barrier, 1, device_id={"gx": gx - 1}, device_id_type=MESH)

    @pl.when(gx < n_gx - 1)
    def _():
        pl.semaphore_signal(barrier, 1, device_id={"gx": gx + 1}, device_id_type=MESH)

    def lanes(t):
        return pl.ds(pl.multiple_of(t * LANES, LANES), LANES)

    def load(t):
        return pltpu.make_async_copy(
            v.at[:, :, :, lanes(t)], win.at[t + 1, :, pl.ds(2, depth), pl.ds(TOP, nrow), :], load_sem.at[t]
        )

    @pl.loop(0, tiles)
    def _(t):
        load(t).start()

    for copy in small:
        copy.wait()
    for b in range(own_blocks):
        at = mine * own_blocks + b
        for c in range(3):
            table[at, c : c + 1, :] = pos[c, b : b + 1, :]
            table[at, 3 + c : 4 + c, :] = bvel[c, b : b + 1, :]
        table[at, 6:7, :] = lift[b : b + 1, :]
        table[at, 7:8, :] = jnp.full((1, pts), turb[b].astype(F32))

    z_gap = jnp.where(gz == 0, 0, depth + 2)

    @pl.loop(0, tiles)
    def _(t):
        for c in range(3):
            for k in range(2):
                win[t + 1, c, z_gap + k, TOP : TOP + nrow, :] = jnp.zeros((nrow, LANES), F32)

    @pl.when(gx == 0)
    def _():
        @pl.loop(0, tiles)
        def _(t):
            win[t + 1, :, 2 : 2 + depth, TOP - 2 : TOP, :] = jnp.zeros((3, depth, 2, LANES), F32)

    @pl.when(gx == n_gx - 1)
    def _():
        @pl.loop(0, tiles)
        def _(t):
            win[t + 1, :, 2 : 2 + depth, TOP + nrow : TOP + nrow + 2, :] = jnp.zeros((3, depth, 2, LANES), F32)

    @pl.when(gy == 0)
    def _():
        win[0, :, 2 : 2 + depth, TOP : TOP + nrow, :] = jnp.zeros((3, depth, nrow, LANES), F32)

    @pl.when(gy == n_gy - 1)
    def _():
        win[tiles + 1, :, 2 : 2 + depth, TOP : TOP + nrow, :] = jnp.zeros((3, depth, nrow, LANES), F32)

    pl.semaphore_wait(barrier, group - 1 + (gx > 0).astype(jnp.int32) + (gx < n_gx - 1).astype(jnp.int32))

    def remote(src, dst, send, recv, device):
        return pltpu.make_async_remote_copy(
            src_ref=src, dst_ref=dst, send_sem=send, recv_sem=recv, device_id=device, device_id_type=MESH
        )

    own_slots = pl.ds(mine * own_blocks, own_blocks)

    def tab(step):
        peer = lax.rem(mine + step, group)
        return remote(
            table.at[own_slots], table.at[own_slots], tab_send.at[step], tab_recv.at[step],
            {"gy": peer // n_gz, "gz": lax.rem(peer, n_gz)},
        )

    z_from = jnp.where(gz == 0, depth - 2, 0)
    z_to = jnp.where(gz == 0, 0, depth + 2)

    def z_copy(t):
        return remote(
            v.at[:, pl.ds(z_from, 2), :, lanes(t)],
            win.at[t + 1, :, pl.ds(z_to, 2), pl.ds(TOP, nrow), :],
            z_send.at[t], z_recv.at[t], {"gz": 1 - gz},
        )

    def x_up(t):
        return remote(
            v.at[:, :, pl.ds(nrow - 2, 2), lanes(t)],
            win.at[t + 1, :, pl.ds(2, depth), pl.ds(TOP - 2, 2), :],
            x_send.at[0, t], x_recv.at[0, t], {"gx": gx + 1},
        )

    def x_down(t):
        return remote(
            v.at[:, :, pl.ds(0, 2), lanes(t)],
            win.at[t + 1, :, pl.ds(2, depth), pl.ds(TOP + nrow, 2), :],
            x_send.at[1, t], x_recv.at[1, t], {"gx": gx - 1},
        )

    def y_copy(side):
        first = 0 if side else ncol - LANES
        return remote(
            v.at[:, :, :, pl.ds(first, LANES)],
            win.at[tiles + 1 if side else 0, :, pl.ds(2, depth), pl.ds(TOP, nrow), :],
            y_send.at[side], y_recv.at[side], {"gy": gy - 1 if side else gy + 1},
        )

    for step in range(1, group):
        tab(step).start()

    @pl.when(gy > 0)
    def _():
        y_copy(1).start()

    @pl.when(gy < n_gy - 1)
    def _():
        y_copy(0).start()

    @pl.loop(0, tiles)
    def _(t):
        @pl.when(gx < n_gx - 1)
        def _():
            x_up(t).start()

        @pl.when(gx > 0)
        def _():
            x_down(t).start()

        z_copy(t).start()

    @pl.loop(0, tiles)
    def _(t):
        load(t).wait()
        high, low = split(win[t + 1, :, 2 : 2 + depth, TOP : TOP + nrow, :].reshape(rows, LANES))
        vhi[t] = high
        vlo[t] = low

    for step in range(1, group):
        tab(step).wait_recv()
    turbine = gy.astype(F32)

    def matches():
        rank = jnp.zeros((8, pts), F32)
        for s in range(blocks):
            entry = table[s]
            match = jnp.broadcast_to(entry[7:8, :], (8, pts)) == turbine
            yield s, entry, [match & (rank == float(k)) for k in range(per_turbine)]
            rank = rank + jnp.where(match, 1.0, 0.0)

    slots = [jnp.zeros((8, pts), F32) for _ in range(per_turbine)]
    for _, entry, chosen in matches():
        slots = [jnp.where(one, entry, held) for one, held in zip(chosen, slots)]

    def flat(row):
        return jnp.concatenate([slot[row : row + 1, :] for slot in slots], axis=1)

    weight_x = gaussian(gx * nrow, nrow, flat(0))
    weight_z = gaussian(gz * depth, depth, flat(2))
    for z in range(depth):
        plane[z * nrow : (z + 1) * nrow, :] = weight_z[z : z + 1, :] * weight_x
    center_y = flat(1)

    per_step = 4
    step_cols = per_step * LANES
    steps = ncol // step_cols

    for j in range(steps):
        at = j * step_cols
        high, low = split(gaussian(gy * ncol + at, step_cols, center_y))
        whi[at : at + step_cols, :] = high
        wlo[at : at + step_cols, :] = low
        vh, vl = (
            jnp.concatenate([term[per_step * j + k] for k in range(per_step)], axis=1) for term in (vhi, vlo)
        )
        dot = functools.partial(jnp.dot, preferred_element_type=F32)
        now = dot(jnp.concatenate([vh, vl], axis=1), jnp.concatenate([high, high], axis=0)) + dot(vh, low)
        if j == 0:
            along[...] = now
        else:
            along[...] += now

    per_comp = depth * nrow
    part[3:8, :] = jnp.zeros((5, count), F32)
    for c in range(3):
        part[c : c + 1, :] = jnp.sum(
            along[c * per_comp : (c + 1) * per_comp, :] * plane[...], axis=0, keepdims=True
        )
    swap = remote(part, other, part_sem.at[0], part_sem.at[1], {"gz": 1 - gz})
    swap.start()
    swap.wait_recv()
    relative = [
        smear_norm * (part[c : c + 1, :] + other[c : c + 1, :]) - flat(3 + c) for c in range(3)
    ]
    speed = jnp.sqrt(relative[0] * relative[0] + relative[1] * relative[1] + relative[2] * relative[2])
    force = [-flat(6) * speed * relative[c] for c in range(3)]

    stacked = [
        jnp.concatenate(
            [force[c][:, k * pts : (k + 1) * pts] for c in range(3)] + [jnp.zeros((5, pts), F32)], axis=0
        )
        for k in range(per_turbine)
    ]
    for s, _, chosen in matches():
        back[s] = sum(jnp.where(one, held, 0.0) for one, held in zip(chosen, stacked))

    def give(step):
        peer = lax.rem(gy + step, n_gy)
        return remote(
            back.at[pl.ds((peer * n_gz + gz) * own_blocks, own_blocks)], owned.at[step],
            back_send.at[step], back_recv.at[step], {"gy": peer},
        )

    for step in range(1, n_gy):
        give(step).start()

    for c in range(3):
        high, low = split((time_step * smear_norm * force[c]) * plane[...])
        ghi[c * per_comp : (c + 1) * per_comp, :] = high
        glo[c * per_comp : (c + 1) * per_comp, :] = low

    @pl.when(gy > 0)
    def _():
        y_copy(0).wait_recv()

    @pl.when(gy < n_gy - 1)
    def _():
        y_copy(1).wait_recv()

    @pl.loop(0, steps)
    def _(j):
        at = pl.multiple_of(j * step_cols, step_cols)
        high, low = whi[pl.ds(at, step_cols), :], wlo[pl.ds(at, step_cols), :]

        def dot(a, b):
            return lax.dot_general(a, b, (((1,), (1,)), ((), ())), preferred_element_type=F32)

        both = jnp.concatenate([ghi[...], glo[...]], axis=1)
        along[...] = dot(both, jnp.concatenate([high, high], axis=1)) + dot(ghi[...], low)
        for k in range(per_step):
            spanwise(win, yd, yl, per_step * j + k)

        @pl.loop(0, per_step)
        def _(k):
            t = per_step * j + k

            @pl.when(gx > 0)
            def _():
                x_up(t).wait_recv()

            @pl.when(gx < n_gx - 1)
            def _():
                x_down(t).wait_recv()

            z_copy(t).wait_recv()
            for z in range(depth):
                body = [
                    along[c * per_comp + z * nrow : c * per_comp + (z + 1) * nrow, lanes(k)]
                    for c in range(3)
                ]
                new = stencil(win, yd, yl, t, z, body)
                for c in range(3):
                    out[c, z, :, lanes(t)] = new[c]

    for step in range(1, n_gy):
        give(step).wait()
    total = back[own_slots] + sum(owned[step] for step in range(1, n_gy))
    for c in range(3):
        for b in range(own_blocks):
            pf[c, b : b + 1, :] = total[b, c : c + 1, :]
    for step in range(1, group):
        tab(step).wait_send()
    swap.wait_send()

    @pl.when(gy > 0)
    def _():
        y_copy(1).wait_send()

    @pl.when(gy < n_gy - 1)
    def _():
        y_copy(0).wait_send()

    @pl.loop(0, tiles)
    def _(t):
        @pl.when(gx < n_gx - 1)
        def _():
            x_up(t).wait_send()

        @pl.when(gx > 0)
        def _():
            x_down(t).wait_send()

        z_copy(t).wait_send()


def write_out(new, forces, new_out, forces_out, sem):
    copies = [pltpu.make_async_copy(forces, forces_out, sem.at[0])]
    for c in range(new.shape[0]):
        copies.append(pltpu.make_async_copy(new.at[c], new_out.at[c], sem.at[c + 1]))
    for copy in copies:
        copy.start()
    for copy in copies:
        copy.wait()


def local(sizes, velocity, blade_pos, block_turbine, blade_vel, lift_coeff):
    n_gx, n_gy, n_gz = sizes
    comps, depth, nrow, ncol = velocity.shape
    own_blocks, _, pts = blade_pos.shape
    tiles = ncol // LANES
    group = n_gy * n_gz
    blocks = group * own_blocks
    count = blocks // n_gy * pts
    rows = comps * depth * nrow
    dma = pltpu.SemaphoreType.DMA
    vmem = pl.BlockSpec(memory_space=pltpu.VMEM)
    by_comp = (blade_pos.shape[1], own_blocks, pts)
    made = pl.pallas_call(
        functools.partial(kernel, sizes),
        out_shape=(pltpu.VMEM(velocity.shape, F32), pltpu.VMEM(by_comp, F32)),
        in_specs=[pl.BlockSpec(memory_space=pl.ANY)] * 5,
        out_specs=(vmem, vmem),
        scratch_shapes=[
            pltpu.VMEM(by_comp, F32),
            pltpu.SMEM((own_blocks,), jnp.int32),
            pltpu.VMEM(by_comp, F32),
            pltpu.VMEM((own_blocks, pts), F32),
            pltpu.VMEM((tiles + 2, comps, depth + 4, nrow + 16, LANES), F32),
            pltpu.VMEM((tiles, rows, LANES), BF16),
            pltpu.VMEM((tiles, rows, LANES), BF16),
            pltpu.VMEM((tiles, depth, comps, nrow, LANES), F32),
            pltpu.VMEM((tiles, depth, comps, nrow, LANES), F32),
            pltpu.VMEM((blocks, 8, pts), F32),
            pltpu.VMEM((ncol, count), BF16),
            pltpu.VMEM((ncol, count), BF16),
            pltpu.VMEM((rows, count), F32),
            pltpu.VMEM((depth * nrow, count), F32),
            pltpu.VMEM((rows, count), BF16),
            pltpu.VMEM((rows, count), BF16),
            pltpu.VMEM((8, count), F32),
            pltpu.VMEM((8, count), F32),
            pltpu.VMEM((blocks, 8, pts), F32),
            pltpu.VMEM((n_gy, own_blocks, 8, pts), F32),
            dma((4,)),
            dma((tiles,)),
            dma((group,)), dma((group,)),
            dma((tiles,)), dma((tiles,)),
            dma((2, tiles)), dma((2, tiles)),
            dma((2,)), dma((2,)),
            dma((2,)),
            dma((n_gy,)), dma((n_gy,)),
        ],
        compiler_params=pltpu.CompilerParams(
            collective_id=0, has_side_effects=True, vmem_limit_bytes=54 * 2**20
        ),
        name="evolve",
    )(
        *(
            pltpu.with_memory_space_constraint(arg, pltpu.HBM)
            for arg in (
                velocity, blade_pos.transpose(1, 0, 2), block_turbine, blade_vel.transpose(1, 0, 2), lift_coeff,
            )
        )
    )
    new, forces = pl.pallas_call(
        write_out,
        out_shape=(jax.ShapeDtypeStruct(velocity.shape, F32), jax.ShapeDtypeStruct(by_comp, F32)),
        in_specs=[vmem, vmem],
        out_specs=(pl.BlockSpec(memory_space=pl.ANY), pl.BlockSpec(memory_space=pl.ANY)),
        scratch_shapes=[dma((comps + 1,))],
        compiler_params=pltpu.CompilerParams(vmem_limit_bytes=16 * 2**20),
        name="write_out",
    )(*made)
    return new, forces.transpose(1, 0, 2)


def solution(mesh):
    sizes = tuple(mesh.shape[axis] for axis in ("gx", "gy", "gz"))
    in_specs = (
        P(None, "gz", "gx", "gy"),
        P(("gx", "gy", "gz"), None, None),
        P(("gx", "gy", "gz")),
        P(("gx", "gy", "gz"), None, None),
        P(("gx", "gy", "gz"), None),
    )
    out_specs = (P(None, "gz", "gx", "gy"), P(("gx", "gy", "gz"), None, None))
    return jax.shard_map(
        functools.partial(local, sizes), mesh=mesh, in_specs=in_specs, out_specs=out_specs, check_vma=False
    )
```
